512 devices in a mesh: notes: 64 (over z, y), tensor: 8 (over x, core).
Axes of the slice: x: 4, y: 4, z: 16, core: 2. Of those that a mesh axis runs over, the one named last changes fastest.
Arguments:
- states: bfloat16 [768, 128, 1024], P('notes', None, 'tensor'), may hold values from -128 to 128
- value_weight: bfloat16 [1024, 1024], P(None, 'tensor'), may hold values from -0.1875 to 0.1875
- latent_query: bfloat16 [16, 1024], P(None, 'tensor'), may hold values from -4 to 4
- patient_ids: int32 [768], P('notes'), may hold values from 0 to 63, as said below
- note_order: int32 [768], P('notes'), may hold values from 0 to 17, as said below
- history_length: int32 [64], P('notes'), may hold values from 1 to 18, as said below
- position_table: bfloat16 [18, 1024], P(None, 'tensor'), may hold values from -3 to 3
- attention_gain: float32 [1024], replicated, may hold values from 0.5 to 1.5
- feedforward_gain: float32 [1024], replicated, may hold values from 0.5 to 1.5
- qkv_weight: bfloat16 [1024, 3, 1024], P(None, None, 'tensor'), may hold values from -2 to 2
- out_weight: bfloat16 [1024, 1024], P('tensor'), may hold values from -0.1875 to 0.1875
- up_weight: bfloat16 [1024, 4096], P(None, 'tensor'), may hold values from -0.1875 to 0.1875
- down_weight: bfloat16 [4096, 1024], P('tensor'), may hold values from -0.09375 to 0.09375
- cotangent: bfloat16 [64, 288, 1024], P('notes', None, 'tensor'), may hold values from -6 to 6
Outputs:
- visit_out: bfloat16 [64, 288, 1024], P('notes', None, 'tensor')
- latent_grads: bfloat16 [768, 16, 1024], P('notes', None, 'tensor')
- value_grad: float32 [1024, 1024], P('notes', 'tensor')
- query_grad: float32 [16, 1024], P(None, 'tensor')
The draws below stay inside these ranges and needn't reach their ends.
Inputs may be any that keep to these rules, and one draw needn't show every extreme that they name: `patient_ids`: patient p's timeline is owned by index p of notes. At most 1 notes held by one index of notes belong to one patient, and some index holds that many for some patient. `note_order`: the notes of patient p carry the numbers 0 to history_length[p] - 1, each once. `history_length`: the lengths sum to 768; the largest is exactly 18.
All inputs are finite; a program needn't handle non-finite values.
Results may differ from the reference program's by a relative error of at most 0.025.
Values may be sent and summed in bfloat16 or wider, within the bound.
A program may use at most 64 MiB of HBM per device.

```python
import jax
import jax.numpy as jnp
from jax import lax

D = 1024
HEADS = 16
HEAD = 64
FF = 4096
LAT = 16
TOK = 128
NOTE_DEV = 12
NOTES = 768
PATIENTS = 64
MOST = 18
HIST = 288
N_NOTES = 64
N_TENSOR = 8


def shared_directions(key):
    inner_key = jax.random.fold_in(key, 101)
    return jnp.clip(jax.random.normal(inner_key, (LAT, D), jnp.float32), -4.0, 4.0)


def route_plan(key):
    inner_key = jax.random.fold_in(key, 202)
    first_key, second_key, third_key, fourth_key = jax.random.split(inner_key, 4)
    shares = jax.random.randint(first_key, (PATIENTS,), 3, 5).astype(jnp.int32)
    shares = shares.at[0].set(0)
    spare = NOTES - MOST - (PATIENTS - 1)
    extra_notes = spare * shares // jnp.sum(shares)
    leftover = spare - jnp.sum(extra_notes)
    line_index = jnp.arange(PATIENTS, dtype=jnp.int32)
    extra_notes = extra_notes + jnp.where((line_index >= 1) & (line_index <= leftover), 1, 0)
    lengths = jnp.where(line_index == 0, MOST, 1 + extra_notes).astype(jnp.int32)
    patient_line = jax.random.permutation(second_key, PATIENTS).astype(jnp.int32)
    line_ends = jnp.cumsum(lengths)
    note_line = jnp.arange(NOTES, dtype=jnp.int32)
    line_place = jnp.sum((note_line[:, None] >= line_ends[None, :]).astype(jnp.int32), axis=1)
    line_starts = line_ends - lengths
    orders = (note_line - line_starts[line_place]).astype(jnp.int32)
    owner_ids = patient_line[line_place]
    device_perm = jax.random.permutation(third_key, PATIENTS).astype(jnp.int32)
    slot_scores = jax.random.randint(fourth_key, (PATIENTS, NOTE_DEV), 0, 65536) * NOTE_DEV + jnp.arange(NOTE_DEV)[None, :]
    slot_perm = jnp.argsort(slot_scores, axis=1, stable=True).astype(jnp.int32)
    residue = note_line % PATIENTS
    device_of = device_perm[residue]
    slot_of = slot_perm[residue, note_line // PATIENTS]
    target = device_of * NOTE_DEV + slot_of
    patient_ids = jnp.zeros((NOTES,), jnp.int32).at[target].set(owner_ids)
    note_order = jnp.zeros((NOTES,), jnp.int32).at[target].set(orders)
    history_length = jnp.zeros((PATIENTS,), jnp.int32).at[patient_line].set(lengths)
    return (patient_ids, note_order, history_length)


def draw_patient_ids(key, part):
    return route_plan(key)[0]


def draw_note_order(key, part):
    return route_plan(key)[1]


def draw_history_length(key, part):
    return route_plan(key)[2]


def draw_latent_query(key, part):
    return shared_directions(key).astype(jnp.bfloat16)


def draw_states(key, part):
    key = jax.random.fold_in(key, 3)
    first_key = jax.random.fold_in(key, 0)
    entries = jnp.clip(jax.random.normal(first_key, (NOTES, TOK, D), jnp.float32), -6.0, 6.0)
    return entries.astype(jnp.bfloat16)


def draw_qkv_weight(key, part):
    key = jax.random.fold_in(key, 5)
    first_key = jax.random.fold_in(key, 0)
    spread = D ** (-0.5)
    entries = jnp.clip(jax.random.normal(first_key, (D, 3, D), jnp.float32), -6.0, 6.0) * spread
    return entries.astype(jnp.bfloat16)


def steps_of(own_key, dims, cuts, low, largest):
    loudness = 1.0
    for dim, blocks in cuts:
        heights = jax.random.uniform(jax.random.fold_in(jax.random.fold_in(own_key, 6), dim), (blocks,), jnp.float32, low / len(cuts), largest / len(cuts))
        loudness = loudness * jnp.repeat(jnp.exp(heights), dims[dim] // blocks).reshape((-1,) + (1,) * (len(dims) - 1 - dim))
    return loudness


def bell_draw(rng, dims, scale, limit, shards=(), held_as=jnp.bfloat16):
    values = scale * jax.random.normal(rng, dims, jnp.float32)
    if shards:
        values = values * steps_of(rng, dims, shards, -0.22, 0.18)
    return jnp.clip(values, -limit, limit).astype(held_as)


def setup_inputs(seed: int = 0) -> dict:
    keys = jax.random.split(jax.random.key(seed), 15)
    states = draw_states(jax.random.fold_in(keys[14], 71), 0)
    value_weight = bell_draw(keys[1], (D, D), D ** -0.5, 0.1875, ((1, 8),))
    latent_query = draw_latent_query(jax.random.fold_in(keys[14], 71), 0)
    patient_ids = draw_patient_ids(jax.random.fold_in(keys[14], 71), 0)
    note_order = draw_note_order(jax.random.fold_in(keys[14], 71), 0)
    history_length = draw_history_length(jax.random.fold_in(keys[14], 71), 0)
    position_table = bell_draw(keys[6], (MOST, D), 0.5, 3.0, ((1, 8),))
    attention_gain = jnp.clip(1.0 + 0.1 * jax.random.normal(keys[7], (D,), jnp.float32), 0.5, 1.5)
    feedforward_gain = jnp.clip(1.0 + 0.1 * jax.random.normal(keys[8], (D,), jnp.float32), 0.5, 1.5)
    qkv_weight = draw_qkv_weight(jax.random.fold_in(keys[14], 71), 0)
    out_weight = bell_draw(keys[10], (D, D), D ** -0.5, 0.1875, ((0, 8),))
    up_weight = bell_draw(keys[11], (D, FF), D ** -0.5, 0.1875, ((1, 8),))
    down_weight = bell_draw(keys[12], (FF, D), FF ** -0.5, 0.09375, ((0, 8),))
    cotangent = bell_draw(keys[13], (PATIENTS, HIST, D), 1.0, 6.0, ((0, 64), (2, 8)))
    return dict(states=states, value_weight=value_weight, latent_query=latent_query, patient_ids=patient_ids, note_order=note_order, history_length=history_length, position_table=position_table, attention_gain=attention_gain, feedforward_gain=feedforward_gain, qkv_weight=qkv_weight, out_weight=out_weight, up_weight=up_weight, down_weight=down_weight, cotangent=cotangent)


EPSILON = 1e-05
MASKED = -1e+30

def rounded(values):
    return lax.optimization_barrier(values.astype(jnp.bfloat16)).astype(jnp.float32)

def norm_rows(values, gain_vector):
    centre = values - lax.optimization_barrier(jnp.mean(values, axis=-1, keepdims=True))
    inverse = lax.rsqrt(lax.optimization_barrier(jnp.mean(centre * centre, axis=-1, keepdims=True)) + EPSILON)
    scaled = centre * inverse
    return (scaled, inverse, (scaled * gain_vector).astype(jnp.bfloat16))

def norm_back(gradient, scaled, inverse, gain_vector):
    weighted = gradient * gain_vector
    centred = weighted - lax.optimization_barrier(jnp.mean(weighted, axis=-1, keepdims=True))
    return inverse * (centred - scaled * lax.optimization_barrier(jnp.mean(weighted * scaled, axis=-1, keepdims=True)))

def group_sum(left_side, right_side):
    partials = jnp.einsum('rgk,gke->gre', left_side.astype(jnp.float32), right_side.astype(jnp.float32))
    return lax.optimization_barrier(jnp.sum(rounded(partials), axis=0))

def pool_block(note_block, value_weight, latent_query):
    notes_here = note_block.shape[0]
    pool_values = jnp.einsum('ntd,dk->ntk', note_block.astype(jnp.float32), value_weight.astype(jnp.float32)).astype(jnp.bfloat16)
    state_heads = note_block.reshape(notes_here, TOK, HEADS, HEAD).astype(jnp.float32)
    value_heads = pool_values.reshape(notes_here, TOK, HEADS, HEAD).astype(jnp.float32)
    query_heads = latent_query.reshape(LAT, HEADS, HEAD).astype(jnp.float32)
    pool_probs = jax.nn.softmax(0.125 * jnp.einsum('lhe,nthe->nhlt', query_heads, state_heads), axis=-1)
    pool_weights = rounded(pool_probs)
    pooled = jnp.einsum('nhlt,nthe->nlhe', pool_weights, value_heads).astype(jnp.bfloat16)
    return (pooled.reshape(notes_here, LAT, D), pool_probs, pool_weights, state_heads, value_heads)

def pool_back(carried, block_items, value_weight, latent_query):
    value_total, query_total = carried
    note_block, grads_block = block_items
    notes_here = note_block.shape[0]
    unused, pool_probs, pool_weights, state_heads, value_heads = pool_block(note_block, value_weight, latent_query)
    grad_heads = grads_block.reshape(notes_here, LAT, HEADS, HEAD).astype(jnp.float32)
    values_grad = jnp.einsum('nhlt,nlhe->nthe', pool_weights, grad_heads).astype(jnp.bfloat16).reshape(notes_here, TOK, D)
    value_total = value_total + jnp.einsum('ntd,ntk->dk', note_block.astype(jnp.float32), values_grad.astype(jnp.float32))
    prob_grad = jnp.einsum('nlhe,nthe->nhlt', grad_heads, value_heads)
    score_grad = rounded(pool_probs * (prob_grad - lax.optimization_barrier(jnp.sum(prob_grad * pool_probs, axis=-1, keepdims=True))))
    query_total = query_total + 0.125 * jnp.einsum('nhlt,nthe->lhe', score_grad, state_heads).reshape(LAT, D)
    return ((value_total, query_total), None)

def visit_patient(patient_items, attention_gain, feedforward_gain, qkv_weight, out_weight, up_weight, down_weight):
    visit_in, cotangent_rows, valid = patient_items
    row_valid = valid[:, None]
    local_width = D // N_TENSOR
    inner_width = FF // N_TENSOR
    scaled_attn, inverse_attn, normed_attn = norm_rows(visit_in.astype(jnp.float32), attention_gain)
    projected = jnp.einsum('rd,djc->rjc', normed_attn.astype(jnp.float32), qkv_weight.astype(jnp.float32)).astype(jnp.bfloat16)
    queries = projected[:, 0].reshape(HIST, HEADS, HEAD).astype(jnp.float32)
    keys_all = projected[:, 1].reshape(HIST, HEADS, HEAD).astype(jnp.float32)
    values_all = projected[:, 2].reshape(HIST, HEADS, HEAD).astype(jnp.float32)
    scores = 0.125 * jnp.einsum('qhe,khe->hqk', queries, keys_all)
    scores = jnp.where(valid[None, None, :], scores, MASKED)
    probs_full = jax.nn.softmax(scores, axis=-1)
    weights_rounded = rounded(probs_full)
    context = jnp.einsum('hqk,khe->qhe', weights_rounded, values_all).astype(jnp.bfloat16)
    attention = group_sum(context.reshape(HIST, N_TENSOR, local_width), out_weight.reshape(N_TENSOR, local_width, D))
    residual = visit_in.astype(jnp.float32) + attention
    scaled_mlp, inverse_mlp, normed_mlp = norm_rows(residual, feedforward_gain)
    upper_proj = jnp.dot(normed_mlp, up_weight, preferred_element_type=jnp.float32)
    hidden = jax.nn.gelu(upper_proj).astype(jnp.bfloat16)
    feedforward = group_sum(hidden.reshape(HIST, N_TENSOR, inner_width), down_weight.reshape(N_TENSOR, inner_width, D))
    visit_out = jnp.where(row_valid, residual + feedforward, 0.0).astype(jnp.bfloat16)
    output_grad = jnp.where(row_valid, cotangent_rows.astype(jnp.float32), 0.0)
    hidden_grad = jnp.dot(output_grad.astype(jnp.bfloat16), down_weight.T, preferred_element_type=jnp.float32)
    unused, gelu_back = jax.vjp(jax.nn.gelu, upper_proj)
    upper_grad = gelu_back(hidden_grad)[0].astype(jnp.bfloat16)
    up_groups = jnp.transpose(up_weight.reshape(D, N_TENSOR, inner_width), (1, 2, 0))
    normed_grad_mlp = group_sum(upper_grad.reshape(HIST, N_TENSOR, inner_width), up_groups)
    residual_grad = output_grad + norm_back(normed_grad_mlp, scaled_mlp, inverse_mlp, feedforward_gain)
    context_grad = jnp.dot(residual_grad.astype(jnp.bfloat16), out_weight.T, preferred_element_type=jnp.float32).astype(jnp.bfloat16)
    grad_heads = context_grad.reshape(HIST, HEADS, HEAD).astype(jnp.float32)
    weight_grad = jnp.einsum('qhe,khe->hqk', grad_heads, values_all)
    values_grad = jnp.einsum('hqk,qhe->khe', weights_rounded, grad_heads).astype(jnp.bfloat16)
    score_grad = rounded(0.125 * probs_full * (weight_grad - lax.optimization_barrier(jnp.sum(weight_grad * probs_full, axis=-1, keepdims=True))))
    queries_grad = jnp.einsum('hqk,khe->qhe', score_grad, keys_all).astype(jnp.bfloat16)
    keys_grad = jnp.einsum('hqk,qhe->khe', score_grad, queries).astype(jnp.bfloat16)
    packed_grad = jnp.stack([queries_grad.reshape(HIST, D), keys_grad.reshape(HIST, D), values_grad.reshape(HIST, D)], axis=1)
    partials = jnp.einsum('rjgf,djgf->grd', packed_grad.reshape(HIST, 3, N_TENSOR, local_width).astype(jnp.float32), qkv_weight.reshape(D, 3, N_TENSOR, local_width).astype(jnp.float32))
    normed_grad_attn = lax.optimization_barrier(jnp.sum(rounded(partials), axis=0))
    visit_grad = residual_grad + norm_back(normed_grad_attn, scaled_attn, inverse_attn, attention_gain)
    return (visit_out, visit_grad.astype(jnp.bfloat16))

def reference(states, value_weight, latent_query, patient_ids, note_order, history_length, position_table, attention_gain, feedforward_gain, qkv_weight, out_weight, up_weight, down_weight, cotangent):
    note_blocks = states.reshape(N_NOTES, NOTE_DEV, TOK, D)
    pooled = lax.map(lambda note_block: pool_block(note_block, value_weight, latent_query)[0], note_blocks).reshape(NOTES, LAT, D)
    latent_line = jnp.arange(LAT, dtype=jnp.int32)
    slot_rows = (patient_ids * HIST + note_order * LAT).astype(jnp.int32)[:, None] + latent_line[None, :]
    placed = jnp.zeros((PATIENTS * HIST, D), jnp.bfloat16).at[slot_rows.reshape(-1)].set(pooled.reshape(NOTES * LAT, D)).reshape(PATIENTS, HIST, D)
    position_rows = jnp.repeat(position_table, LAT, axis=0).astype(jnp.float32)
    valid = jnp.arange(HIST, dtype=jnp.int32)[None, :] < (history_length * LAT)[:, None]
    visit_in = jnp.where(valid[:, :, None], placed.astype(jnp.float32) + position_rows[None], 0.0).astype(jnp.bfloat16)
    visit_out, visit_grad = lax.map(lambda patient_items: visit_patient(patient_items, attention_gain, feedforward_gain, qkv_weight, out_weight, up_weight, down_weight), (visit_in, cotangent, valid))
    latent_grads = visit_grad[patient_ids[:, None], (note_order * LAT).astype(jnp.int32)[:, None] + latent_line[None, :]]
    grad_blocks = latent_grads.reshape(N_NOTES, NOTE_DEV, LAT, D)
    starting = (jnp.zeros((D, D), jnp.float32), jnp.zeros((LAT, D), jnp.float32))
    totals, unused = lax.scan(lambda carried, block_items: pool_back(carried, block_items, value_weight, latent_query), starting, (note_blocks, grad_blocks))
    return (visit_out, latent_grads, totals[0], totals[1])
```

```python
import functools

import jax
import jax.numpy as jnp
from jax import lax
from jax.experimental import pallas as pl
from jax.experimental.pallas import tpu as pltpu
from jax.sharding import PartitionSpec as P

HEAD = 64
EPSILON = 1e-05
MASKED = -1e30
MESH = pl.DeviceIdType.MESH
F32 = jnp.float32
BF16 = jnp.bfloat16
I32 = jnp.int32


def remote(src, dst, send, recv, device):
    return pltpu.make_async_remote_copy(
        src_ref=src,
        dst_ref=dst,
        send_sem=send,
        recv_sem=recv,
        device_id=device,
        device_id_type=MESH,
    )


def dot_nn(a, b):
    return lax.dot_general(a, b, (((1,), (0,)), ((), ())), preferred_element_type=F32)


def dot_nt(a, b):
    return lax.dot_general(a, b, (((1,), (1,)), ((), ())), preferred_element_type=F32)


def dot_tn(a, b):
    return lax.dot_general(a, b, (((0,), (0,)), ((), ())), preferred_element_type=F32)


def iota(shape, dim):
    return lax.broadcasted_iota(I32, shape, dim)


class Place:
    def __init__(self, nt):
        self.nt = nt
        self.nx = nt // 2
        self.me = lax.axis_index("tensor")
        self.x = self.me // 2
        self.c = lax.rem(self.me, 2)
        self.sibling = self.at(0, 1)

    def at(self, step, flip):
        core = 1 - self.c if flip else self.c
        return lax.rem(self.x + step, self.nx) * 2 + core


class RingGather:
    def __init__(self, place, src, full, send, recv):
        self.place, self.src, self.full, self.send, self.recv = place, src, full, send, recv
        self.half = src.shape[0] // 2
        self.copies = []

    def part(self, ref, j):
        return ref.at[pl.ds(j * self.half, self.half)]

    def copy(self, src, owner, j, to):
        one = remote(
            src,
            self.part(self.full.at[owner], j),
            self.send.at[len(self.copies)],
            self.recv.at[owner, j],
            {"tensor": to},
        )
        one.start()
        self.copies.append(one)

    def arrive(self, owner, j):
        remote(
            self.part(self.src, j),
            self.part(self.full.at[owner], j),
            self.send.at[0],
            self.recv.at[owner, j],
            {"tensor": owner},
        ).wait_recv()

    def start(self):
        p = self.place
        right, left = p.at(1, 0), p.at(3, 0)
        for j, to in ((0, right), (1, left), (1, right), (0, left), (0, p.sibling), (1, p.sibling)):
            self.copy(self.part(self.src, j), p.me, j, to)
        self.full[p.me] = self.src[...]

    def pass_on(self):
        p = self.place
        right, left = p.at(1, 0), p.at(3, 0)
        for owner, j, to in ((left, 0, right), (right, 1, left)):
            self.arrive(owner, j)
            self.copy(self.part(self.full.at[owner], j), owner, j, to)
            self.copy(self.part(self.full.at[owner], j), owner, j, p.sibling)

    def relay_near(self):
        p = self.place
        for owner, j in ((p.at(3, 0), 1), (p.at(1, 0), 0)):
            self.arrive(owner, j)
            self.copy(self.part(self.full.at[owner], j), owner, j, p.sibling)

    def relay_far(self):
        p = self.place
        for j in range(2):
            self.arrive(p.at(2, 0), j)
            self.copy(self.part(self.full.at[p.at(2, 0)], j), p.at(2, 0), j, p.sibling)

    def finish(self):
        for step in (0, 1, 3, 2):
            for j in range(2):
                self.arrive(self.place.at(step, 1), j)
        for one in self.copies:
            one.wait_send()


class RelayGather:
    def __init__(self, place, src, full, send, recv):
        self.place, self.src, self.full, self.send, self.recv = place, src, full, send, recv
        self.copies = []

    def copy(self, src, owner, to):
        one = remote(
            src,
            self.full.at[owner],
            self.send.at[len(self.copies)],
            self.recv.at[owner],
            {"tensor": to},
        )
        one.start()
        self.copies.append(one)

    def arrive(self, owner):
        remote(
            self.src, self.full.at[owner], self.send.at[0], self.recv.at[owner], {"tensor": owner}
        ).wait_recv()

    def start(self):
        p = self.place
        for to in (p.at(2, 0), p.at(1, 0), p.at(3, 0), p.sibling):
            self.copy(self.src, p.me, to)
        self.full[p.me] = self.src[...]

    def finish(self):
        p = self.place
        for step in (1, 3, 2):
            owner = p.at(step, 0)
            self.arrive(owner)
            self.copy(self.full.at[owner], owner, p.sibling)
        for step in (0, 1, 3, 2):
            self.arrive(p.at(step, 1))

    def drain(self):
        for one in self.copies:
            one.wait_send()


class Exchange:
    def __init__(self, place, src, slots, send, recv, same=False):
        self.place, self.src, self.slots, self.send, self.recv = place, src, slots, send, recv
        self.copies = []
        self.same = same

    def block(self, t):
        return self.src if self.same else self.src.at[t]

    def start(self):
        p = self.place
        for k in range(1, p.nt):
            to = lax.rem(p.me + k, p.nt)
            one = remote(
                self.block(to),
                self.slots.at[p.me],
                self.send.at[k - 1],
                self.recv.at[p.me],
                {"tensor": to},
            )
            one.start()
            self.copies.append(one)
        self.slots[p.me] = self.block(p.me)[...]

    def finish(self):
        p = self.place
        for k in range(1, p.nt):
            owner = lax.rem(p.me + k, p.nt)
            remote(
                self.block(owner),
                self.slots.at[owner],
                self.send.at[0],
                self.recv.at[owner],
                {"tensor": owner},
            ).wait_recv()

    def drain(self):
        for one in self.copies:
            one.wait_send()


class AllToAll:
    def __init__(self, count, src, slots, send, recv):
        self.count, self.src, self.slots, self.send, self.recv = count, src, slots, send, recv
        self.me = lax.axis_index("notes")

    def start(self):
        def step(k, carry):
            to = lax.rem(self.me + k, self.count)
            remote(
                self.src.at[to], self.slots.at[self.me], self.send, self.recv, {"notes": to}
            ).start()
            return carry

        lax.fori_loop(1, self.count, step, 0)
        self.slots[self.me] = self.src[self.me]

    def finish(self):
        span = pl.ds(0, self.count - 1)
        remote(
            self.src.at[span], self.slots.at[span], self.send, self.recv, {"notes": self.me}
        ).wait()


def norm_rows(values, gain):
    centre = values - jnp.mean(values, axis=-1, keepdims=True)
    inverse = lax.rsqrt(jnp.mean(centre * centre, axis=-1, keepdims=True) + EPSILON)
    scaled = centre * inverse
    return scaled, inverse, (scaled * gain).astype(BF16)


def side_by_side(blocks):
    return jnp.concatenate([blocks[t] for t in range(blocks.shape[0])], axis=1)


def body(
    dims,
    pid,
    order,
    length,
    states,
    lq,
    pos,
    gain1,
    gain2,
    cot,
    outw,
    wv_hbm,
    qkv_hbm,
    up_hbm,
    down_hbm,
    visit_out,
    latent_out,
    value_out,
    query_out,
    wv,
    qkv,
    up,
    down,
    full,
    cotf,
    outf,
    codes_out,
    codes_in,
    probs,
    weights,
    values,
    mixture,
    slots,
    arrived,
    place_t,
    place,
    vloc,
    visitf,
    scaled1,
    inverse1,
    projected,
    vprobs,
    ctxl,
    ctxf,
    residual_own,
    hidden_grad,
    part2,
    got2,
    sum2,
    sum2f,
    partf,
    gotf,
    rgrad,
    part1,
    got1,
    stat,
    stats,
    slots2,
    arrived2,
    vpart,
    vgot,
    vpart2,
    vgot2,
    qpart,
    qgot,
    qpart2,
    qgot2,
    load_sem,
    ring_send,
    ring_recv,
    relay_send,
    relay_recv,
    ex_send,
    ex_recv,
    a2a_send,
    a2a_recv,
    y_send,
    y_recv,
    z_send,
    z_recv,
):
    nn, ny, nt, notes, tok, lat, most = dims
    nz = nn // ny
    rows = most * lat
    width = 128
    tp = Place(nt)
    who = lax.axis_index("notes")
    wz, wy = who // ny, lax.rem(who, ny)

    barrier = pltpu.get_barrier_semaphore()

    def greet(k, carry):
        pl.semaphore_signal(
            barrier, inc=1, device_id={"notes": lax.rem(who + k, nn)}, device_id_type=MESH
        )
        return carry

    for k in range(1, nt):
        pl.semaphore_signal(
            barrier, inc=1, device_id={"tensor": lax.rem(tp.me + k, nt)}, device_id_type=MESH
        )
    lax.fori_loop(1, nn, greet, 0)
    loads = [
        pltpu.make_async_copy(src, dst, load_sem.at[i])
        for i, (src, dst) in enumerate(((wv_hbm, wv), (qkv_hbm, qkv), (up_hbm, up), (down_hbm, down)))
    ]
    for one in loads:
        one.start()
    pl.semaphore_wait(barrier, nt - 1 + nn - 1)

    ring_states = RingGather(tp, states, full, ring_send.at[0], ring_recv.at[0])
    ring_cot = RingGather(tp, cot, cotf, ring_send.at[1], ring_recv.at[1])
    ring_out = RingGather(tp, outw, outf, ring_send.at[2], ring_recv.at[2])
    ring_states.start()

    patient = iota((nn, 1, width), 0)
    codes = jnp.zeros((nn, 1, width), I32)
    for n in range(notes):
        codes = jnp.where(patient == pid[n], order[n] + 1, codes)
    codes_out[...] = codes
    route = AllToAll(nn, codes_out, codes_in, a2a_send.at[0], a2a_recv.at[0])
    route.start()

    low = (iota((1, width), 1) < HEAD).astype(F32)
    low_b, high_b = low.astype(BF16), (1.0 - low).astype(BF16)
    query = jnp.concatenate([lq[...] * low_b, lq[...] * high_b], axis=0)
    both = 2 * lat
    for n in range(notes):
        score = 0.125 * dot_nt(query, states[n * tok : (n + 1) * tok, :])
        score = jnp.exp(score - jnp.max(score, axis=-1, keepdims=True))
        prob = score / jnp.sum(score, axis=-1, keepdims=True)
        probs[n * both : (n + 1) * both, :] = prob
        weights[n * both : (n + 1) * both, :] = prob.astype(BF16)

    ring_states.pass_on()
    ring_states.relay_near()
    ring_cot.start()
    ring_out.start()
    ring_states.relay_far()
    ring_states.finish()

    loads[0].wait()
    pooled = []
    lane_low = iota((lat, width), 1) < HEAD
    for n in range(notes):
        here = pl.ds(n * tok, tok)
        note = jnp.concatenate([full[t, here, :] for t in range(nt)], axis=1)
        value = dot_nn(note, wv[...]).astype(BF16)
        values[here, :] = value
        mix = dot_nn(weights[n * both : (n + 1) * both, :], value)
        pooled.append(jnp.where(lane_low, mix[:lat], mix[lat:]))
    pooled = jnp.concatenate(pooled, axis=0).astype(BF16)

    line = iota((1, notes * lat), 1)
    target = lax.rem(line, lat)
    for n in range(notes):
        target = jnp.where(line // lat == n, target + pid[n] * lat, target)
    select = (iota((nn * lat, notes * lat), 0) == target).astype(F32).astype(BF16)
    slots[...] = dot_nn(select, pooled).astype(BF16).reshape(nn, lat, width)
    forward = AllToAll(nn, slots, arrived, a2a_send.at[1], a2a_recv.at[1])
    forward.start()

    ring_cot.pass_on()
    ring_out.pass_on()
    ring_cot.relay_near()
    ring_out.relay_near()
    ring_cot.relay_far()
    ring_out.relay_far()

    route.finish()
    code = jnp.broadcast_to(codes_in[...], (nn, lat, width)).reshape(nn * lat, width)
    slot_row = jnp.where(code > 0, (code - 1) * lat + lax.rem(iota((nn * lat, width), 0), lat), -1)
    padded = place_t.shape[1]
    placing = jnp.concatenate(
        [
            (iota((nn * lat, width), 1) + j * width == slot_row).astype(F32)
            for j in range(padded // width)
        ],
        axis=1,
    )
    place_t[...] = placing.astype(BF16)
    place[...] = jnp.transpose(placing).astype(BF16)

    for n in range(notes):
        here = pl.ds(n * tok, tok)
        note = jnp.concatenate([full[t, here, :] for t in range(nt)], axis=1)
        mixed = dot_nn(weights[n * both : (n + 1) * both, :], note)
        mixture[n * both : (n + 1) * both, :] = mixed.astype(BF16)

    limit = length[0] * lat
    row_valid = iota((rows, width), 0) < limit
    positions = pos[...].astype(F32)
    positions = jnp.concatenate(
        [jnp.broadcast_to(positions[m : m + 1, :], (lat, width)) for m in range(most)], axis=0
    )
    ring_cot.finish()
    ring_out.finish()
    loads[1].wait()
    loads[2].wait()
    loads[3].wait()
    out_grad = jnp.where(iota((rows, nt * width), 0) < limit, side_by_side(cotf).astype(F32), 0.0)
    hidden_grad[...] = dot_nt(out_grad.astype(BF16), down[...])

    forward.finish()
    placed = dot_nn(place[...], arrived[...].reshape(nn * lat, width))[:rows]
    vloc[...] = jnp.where(row_valid, placed + positions, 0.0).astype(BF16)

    gather1 = RelayGather(tp, vloc, visitf, relay_send.at[0], relay_recv.at[0])
    gather1.start()
    gather1.finish()
    visit = side_by_side(visitf).astype(F32)
    scaled, inverse, normed = norm_rows(visit, gain1[...])
    scaled1[...] = scaled
    inverse1[...] = jnp.broadcast_to(inverse, (rows, width))
    projected[...] = dot_nn(normed, qkv[...]).astype(BF16)
    q, k, v = (projected[:, j * width : (j + 1) * width] for j in range(3))
    key_valid = iota((1, rows), 1) < limit
    contexts = []
    for h, mask in enumerate((low_b, high_b)):
        score = jnp.where(key_valid, 0.125 * dot_nt(q, k * mask), MASKED)
        score = jnp.exp(score - jnp.max(score, axis=-1, keepdims=True))
        prob = score / jnp.sum(score, axis=-1, keepdims=True)
        vprobs[h] = prob
        contexts.append(dot_nn(prob.astype(BF16), v))
    row_low = iota((rows, width), 1) < HEAD
    ctxl[...] = jnp.where(row_low, contexts[0], contexts[1]).astype(BF16)

    gather2 = RelayGather(tp, ctxl, ctxf, relay_send.at[1], relay_recv.at[1])
    gather2.start()
    gather2.finish()
    attention = dot_nn(side_by_side(ctxf), outf[...].reshape(nt * width, nt * width))
    residual = side_by_side(visitf).astype(F32) + attention
    scaled2, inverse2, normed2 = norm_rows(residual, gain2[...])
    rgrad[...] = residual
    own = pl.ds(pl.multiple_of(tp.me * width, width), width)
    residual_own[...] = rgrad[:, own]
    upper = dot_nn(normed2, up[...])
    cubic = 0.7978845608028654 * (upper + 0.044715 * upper * upper * upper)
    bend = jnp.tanh(cubic)
    hidden = (0.5 * upper * (1.0 + bend)).astype(BF16)
    slope = 0.5 * (1.0 + bend) + 0.5 * upper * (1.0 - bend * bend) * (
        0.7978845608028654 * (1.0 + 3.0 * 0.044715 * upper * upper)
    )
    upper_grad = (hidden_grad[...] * slope).astype(BF16)
    for t in range(nt):
        part2[t] = dot_nt(upper_grad, up[t * width : (t + 1) * width, :]).astype(BF16)
    reduce2 = Exchange(tp, part2, got2, ex_send.at[0], ex_recv.at[0])
    reduce2.start()
    for t in range(nt):
        partf[t] = dot_nn(hidden, down[:, t * width : (t + 1) * width]).astype(BF16)
    reduce2.finish()
    total = got2[0].astype(F32)
    for t in range(1, nt):
        total = total + got2[t].astype(F32)
    sum2[...] = total.astype(BF16)
    gather3 = RelayGather(tp, sum2, sum2f, relay_send.at[2], relay_recv.at[2])
    gather3.start()
    reducef = Exchange(tp, partf, gotf, ex_send.at[1], ex_recv.at[1])
    gather3.finish()
    reducef.start()

    weighted = side_by_side(sum2f).astype(F32) * gain2[...]
    centred = weighted - jnp.mean(weighted, axis=-1, keepdims=True)
    out_grad = jnp.where(iota((rows, nt * width), 0) < limit, side_by_side(cotf).astype(F32), 0.0)
    residual_grad = out_grad + inverse2 * (
        centred - scaled2 * jnp.mean(weighted * scaled2, axis=-1, keepdims=True)
    )
    rgrad[...] = residual_grad
    context_grad = dot_nt(residual_grad.astype(BF16), outw[...]).astype(BF16)

    q, k, v = (projected[:, j * width : (j + 1) * width] for j in range(3))
    query_grads, key_grads, value_grads = [], [], []
    for h, mask in enumerate((low_b, high_b)):
        prob = vprobs[h]
        weight_grad = dot_nt(context_grad, v * mask)
        value_grads.append(dot_tn(prob.astype(BF16), context_grad))
        score_grad = (
            0.125 * prob * (weight_grad - jnp.sum(weight_grad * prob, axis=-1, keepdims=True))
        ).astype(BF16)
        query_grads.append(dot_nn(score_grad, k))
        key_grads.append(dot_tn(score_grad, q))
    packed = jnp.concatenate(
        [
            jnp.where(row_low, pair[0], pair[1]).astype(BF16)
            for pair in (query_grads, key_grads, value_grads)
        ],
        axis=1,
    )
    first_sum = jnp.zeros((rows, 1), F32)
    second_sum = jnp.zeros((rows, 1), F32)
    for t in range(nt):
        cols = slice(t * width, (t + 1) * width)
        partial = dot_nt(packed, qkv[cols, :])
        part1[t] = partial.astype(BF16)
        weighted = partial * gain1[:, cols]
        first_sum = first_sum + jnp.sum(weighted, axis=-1, keepdims=True)
        second_sum = second_sum + jnp.sum(weighted * scaled1[:, cols], axis=-1, keepdims=True)
    reduce1 = Exchange(tp, part1, got1, ex_send.at[2], ex_recv.at[2])
    reduce1.start()
    lane = iota((rows, width), 1)
    both_sums = jnp.where(lane == 0, first_sum, jnp.where(lane == 1, second_sum, 0.0))
    stat[...] = jnp.transpose(
        jnp.concatenate([both_sums, jnp.zeros((padded - rows, width), F32)], axis=0)
    )[:8]
    gather4 = Exchange(tp, stat, stats, ex_send.at[3], ex_recv.at[3], same=True)
    gather4.start()
    reduce1.finish()
    gather4.finish()
    total = got1[0].astype(F32)
    means = stats[0]
    for t in range(1, nt):
        total = total + got1[t].astype(F32)
        means = means + stats[t]
    means = jnp.transpose(
        jnp.concatenate([means, jnp.zeros((width - 8, padded), F32)], axis=0)
    )[:rows] * (1.0 / (nt * width))
    visit_grad = rgrad[:, own] + inverse1[...] * (
        total * gain1[:, own] - means[:, 0:1] - scaled1[:, own] * means[:, 1:2]
    )
    visit_grad = visit_grad.astype(BF16)
    slots2[...] = dot_nn(place_t[:, :rows], visit_grad).astype(BF16).reshape(nn, lat, width)
    back = AllToAll(nn, slots2, arrived2, a2a_send.at[2], a2a_recv.at[2])
    back.start()

    reducef.finish()
    total = gotf[0].astype(F32)
    for t in range(1, nt):
        total = total + gotf[t].astype(F32)
    visit_out[...] = jnp.where(row_valid, residual_own[...] + total, 0.0).astype(BF16)
    sublane = iota((notes * lat, nn * lat), 0)
    wanted = jnp.zeros((notes * lat, 1), I32)
    column = iota((notes * lat, 1), 0)
    wanted = lax.rem(column, lat)
    for n in range(notes):
        wanted = jnp.where(column // lat == n, wanted + pid[n] * lat, wanted)
    unselect = (iota((notes * lat, nn * lat), 1) == wanted).astype(F32).astype(BF16)
    for gather in (gather1, gather2, gather3):
        gather.drain()
    for exchange in (reduce2, reducef, reduce1, gather4):
        exchange.drain()

    back.finish()
    latent = dot_nn(unselect, arrived2[...].reshape(nn * lat, width)).astype(BF16)
    latent_out[...] = latent
    halves = (latent * low_b, latent * high_b)
    spread = jnp.concatenate(
        [half[n * lat : (n + 1) * lat] for n in range(notes) for half in halves], axis=0
    )
    partial = dot_tn(mixture[...], spread).astype(BF16)
    vpart[...] = partial.reshape(nz, ny, lat, width)
    query_total = jnp.zeros((both, width), F32)
    for n in range(notes):
        here = slice(n * both, (n + 1) * both)
        tokens = slice(n * tok, (n + 1) * tok)
        prob = probs[here, :]
        prob_grad = dot_nt(spread[here], values[tokens, :])
        score_grad = prob * (prob_grad - jnp.sum(prob_grad * prob, axis=-1, keepdims=True))
        query_total = query_total + dot_nn(score_grad.astype(BF16), states[tokens, :])
    qpart[...] = 0.125 * jnp.where(lane_low, query_total[:lat], query_total[lat:])

    y_copies = []
    for s in range(1, ny):
        to = lax.rem(wy + s, ny)
        device = {"notes": wz * ny + to}
        for i, (src, dst) in enumerate(((vpart.at[:, to], vgot.at[wy]), (qpart, qgot.at[wy]))):
            one = remote(src, dst, y_send.at[i, s], y_recv.at[i, wy], device)
            one.start()
            y_copies.append(one)
    total = vpart[:, wy].astype(F32)
    query_sum = qpart[...]
    for s in range(1, ny):
        owner = lax.rem(wy + s, ny)
        device = {"notes": wz * ny + owner}
        for i, (src, dst) in enumerate(((vpart.at[:, owner], vgot.at[owner]), (qpart, qgot.at[owner]))):
            remote(src, dst, y_send.at[i, s], y_recv.at[i, owner], device).wait_recv()
        total = total + vgot[owner].astype(F32)
        query_sum = query_sum + qgot[owner]
    vpart2[...] = total.astype(BF16)
    qpart2[...] = query_sum

    def along_z(k, carry):
        to = lax.rem(wz + k, nz)
        device = {"notes": to * ny + wy}
        remote(vpart2.at[to], vgot2.at[wz], z_send.at[0], z_recv.at[0], device).start()
        remote(qpart2, qgot2.at[wz], z_send.at[1], z_recv.at[1], device).start()
        return carry

    lax.fori_loop(1, nz, along_z, 0)
    vgot2[wz] = vpart2[wz]
    qgot2[wz] = qpart2[...]
    for one in y_copies:
        one.wait_send()
    span = pl.ds(0, nz - 1)
    remote(vpart2.at[span], vgot2.at[span], z_send.at[0], z_recv.at[0], {"notes": who}).wait()
    remote(qgot2.at[span], qgot2.at[span], z_send.at[1], z_recv.at[1], {"notes": who}).wait()
    total = vgot2[0].astype(F32)
    query_sum = qgot2[0]
    for z in range(1, nz):
        total = total + vgot2[z].astype(F32)
        query_sum = query_sum + qgot2[z]
    value_out[...] = total
    query_out[...] = query_sum


def shards(
    mesh_shape,
    states,
    value_weight,
    latent_query,
    patient_ids,
    note_order,
    history_length,
    position_table,
    attention_gain,
    feedforward_gain,
    qkv_weight,
    out_weight,
    up_weight,
    down_weight,
    cotangent,
):
    nn, nt = mesh_shape["notes"], mesh_shape["tensor"]
    ny = 4
    nz = nn // ny
    notes, tok, width = states.shape
    lat, most = latent_query.shape[0], position_table.shape[0]
    rows = most * lat
    dim = nt * width
    inner = up_weight.shape[1]
    padded = -(-rows // 128) * 128
    both = 2 * lat
    dims = (nn, ny, nt, notes, tok, lat, most)
    vmem = pl.BlockSpec(memory_space=pltpu.VMEM)
    smem = pl.BlockSpec(memory_space=pltpu.SMEM)
    hbm = pl.BlockSpec(memory_space=pl.ANY)
    V = pltpu.VMEM
    dma = pltpu.SemaphoreType.DMA
    block = (nt, rows, width)
    scratch = [
        V((dim, width), BF16),
        V((dim, 3 * width), BF16),
        V((dim, inner), BF16),
        V((inner, dim), BF16),
        V((nt, notes * tok, width), BF16),
        V(block, BF16),
        V((nt, width, dim), BF16),
        V((nn, 1, width), I32),
        V((nn, 1, width), I32),
        V((notes * both, tok), F32),
        V((notes * both, tok), BF16),
        V((notes * tok, width), BF16),
        V((notes * both, dim), BF16),
        V((nn, lat, width), BF16),
        V((nn, lat, width), BF16),
        V((nn * lat, padded), BF16),
        V((padded, nn * lat), BF16),
        V((rows, width), BF16),
        V(block, BF16),
        V((rows, dim), F32),
        V((rows, width), F32),
        V((rows, 3 * width), BF16),
        V((2, rows, rows), F32),
        V((rows, width), BF16),
        V(block, BF16),
        V((rows, width), F32),
        V((rows, inner), F32),
        V(block, BF16),
        V(block, BF16),
        V((rows, width), BF16),
        V(block, BF16),
        V(block, BF16),
        V(block, BF16),
        V((rows, dim), F32),
        V(block, BF16),
        V(block, BF16),
        V((8, padded), F32),
        V((nt, 8, padded), F32),
        V((nn, lat, width), BF16),
        V((nn, lat, width), BF16),
        V((nz, ny, lat, width), BF16),
        V((ny, nz, lat, width), BF16),
        V((nz, lat, width), BF16),
        V((nz, lat, width), BF16),
        V((lat, width), F32),
        V((ny, lat, width), F32),
        V((lat, width), F32),
        V((nz, lat, width), F32),
        dma((4,)),
        dma((3, 14)),
        dma((3, nt, 2)),
        dma((3, 7)),
        dma((3, nt)),
        dma((4, nt - 1)),
        dma((4, nt)),
        dma((3,)),
        dma((3,)),
        dma((2, ny)),
        dma((2, ny)),
        dma((2,)),
        dma((2,)),
    ]
    visit_out, latent_grads, value_grad, query_grad = pl.pallas_call(
        functools.partial(body, dims),
        out_shape=(
            jax.ShapeDtypeStruct((rows, width), BF16),
            jax.ShapeDtypeStruct((notes * lat, width), BF16),
            jax.ShapeDtypeStruct((dim // nn, width), F32),
            jax.ShapeDtypeStruct((lat, width), F32),
        ),
        in_specs=[smem] * 3 + [vmem] * 7 + [hbm] * 4,
        out_specs=(vmem,) * 4,
        scratch_shapes=scratch,
        name="note_visit_step",
        compiler_params=pltpu.CompilerParams(
            collective_id=0, has_side_effects=True, vmem_limit_bytes=56 * 2**20
        ),
    )(
        patient_ids,
        note_order,
        history_length,
        states.reshape(notes * tok, width),
        latent_query,
        position_table,
        attention_gain.reshape(1, dim),
        feedforward_gain.reshape(1, dim),
        cotangent.reshape(rows, width),
        out_weight,
        value_weight,
        qkv_weight.reshape(dim, 3 * width),
        up_weight,
        down_weight,
    )
    return (
        visit_out[None],
        latent_grads.reshape(notes, lat, width),
        value_grad,
        query_grad,
    )


def solution(mesh):
    return jax.shard_map(
        functools.partial(shards, dict(mesh.shape)),
        mesh=mesh,
        in_specs=(
            P("notes", None, "tensor"),
            P(None, "tensor"),
            P(None, "tensor"),
            P("notes"),
            P("notes"),
            P("notes"),
            P(None, "tensor"),
            P(),
            P(),
            P(None, None, "tensor"),
            P("tensor", None),
            P(None, "tensor"),
            P("tensor", None),
            P("notes", None, "tensor"),
        ),
        out_specs=(
            P("notes", None, "tensor"),
            P("notes", None, "tensor"),
            P("notes", "tensor"),
            P(None, "tensor"),
        ),
        check_vma=False,
    )
```

```python
import functools

import jax
import jax.numpy as jnp
from jax import lax
from jax.experimental import pallas as pl
from jax.experimental.pallas import tpu as pltpu
from jax.sharding import PartitionSpec as P

HEAD = 64
EPSILON = 1e-05
MASKED = -1e30
MESH = pl.DeviceIdType.MESH
F32 = jnp.float32
BF16 = jnp.bfloat16
I32 = jnp.int32


def remote(src, dst, send, recv, device):
    return pltpu.make_async_remote_copy(
        src_ref=src,
        dst_ref=dst,
        send_sem=send,
        recv_sem=recv,
        device_id=device,
        device_id_type=MESH,
    )


def dot_nn(a, b):
    return lax.dot_general(a, b, (((1,), (0,)), ((), ())), preferred_element_type=F32)


def dot_nt(a, b):
    return lax.dot_general(a, b, (((1,), (1,)), ((), ())), preferred_element_type=F32)


def dot_tn(a, b):
    return lax.dot_general(a, b, (((0,), (0,)), ((), ())), preferred_element_type=F32)


def iota(shape, dim):
    return lax.broadcasted_iota(I32, shape, dim)


class Place:
    def __init__(self, nt):
        self.nt = nt
        self.nx = nt // 2
        self.me = lax.axis_index("tensor")
        self.x = self.me // 2
        self.c = lax.rem(self.me, 2)
        self.sibling = self.at(0, 1)

    def at(self, step, flip):
        core = 1 - self.c if flip else self.c
        return lax.rem(self.x + step, self.nx) * 2 + core


class RingGather:
    def __init__(self, place, src, full, send, recv):
        self.place, self.src, self.full, self.send, self.recv = place, src, full, send, recv
        self.half = src.shape[0] // 2
        self.copies = []

    def part(self, ref, j):
        return ref.at[pl.ds(j * self.half, self.half)]

    def copy(self, src, owner, j, to):
        one = remote(
            src,
            self.part(self.full.at[owner], j),
            self.send.at[len(self.copies)],
            self.recv.at[owner, j],
            {"tensor": to},
        )
        one.start()
        self.copies.append(one)

    def arrive(self, owner, j):
        remote(
            self.part(self.src, j),
            self.part(self.full.at[owner], j),
            self.send.at[0],
            self.recv.at[owner, j],
            {"tensor": owner},
        ).wait_recv()

    def start(self):
        p = self.place
        right, left = p.at(1, 0), p.at(3, 0)
        for j, to in ((0, right), (1, left), (1, right), (0, left), (0, p.sibling), (1, p.sibling)):
            self.copy(self.part(self.src, j), p.me, j, to)
        self.full[p.me] = self.src[...]

    def pass_on(self):
        p = self.place
        right, left = p.at(1, 0), p.at(3, 0)
        for owner, j, to in ((left, 0, right), (right, 1, left)):
            self.arrive(owner, j)
            self.copy(self.part(self.full.at[owner], j), owner, j, to)
            self.copy(self.part(self.full.at[owner], j), owner, j, p.sibling)

    def relay_near(self):
        p = self.place
        for owner, j in ((p.at(3, 0), 1), (p.at(1, 0), 0)):
            self.arrive(owner, j)
            self.copy(self.part(self.full.at[owner], j), owner, j, p.sibling)

    def relay_far(self):
        p = self.place
        for j in range(2):
            self.arrive(p.at(2, 0), j)
            self.copy(self.part(self.full.at[p.at(2, 0)], j), p.at(2, 0), j, p.sibling)

    def finish(self):
        for step in (0, 1, 3, 2):
            for j in range(2):
                self.arrive(self.place.at(step, 1), j)
        for one in self.copies:
            one.wait_send()


class RelayGather:
    def __init__(self, place, src, full, send, recv):
        self.place, self.src, self.full, self.send, self.recv = place, src, full, send, recv
        self.copies = []

    def copy(self, src, owner, to):
        one = remote(
            src,
            self.full.at[owner],
            self.send.at[len(self.copies)],
            self.recv.at[owner],
            {"tensor": to},
        )
        one.start()
        self.copies.append(one)

    def arrive(self, owner):
        remote(
            self.src, self.full.at[owner], self.send.at[0], self.recv.at[owner], {"tensor": owner}
        ).wait_recv()

    def start(self):
        p = self.place
        for to in (p.at(2, 0), p.at(1, 0), p.at(3, 0), p.sibling):
            self.copy(self.src, p.me, to)
        self.full[p.me] = self.src[...]

    def finish(self):
        p = self.place
        for step in (1, 3, 2):
            owner = p.at(step, 0)
            self.arrive(owner)
            self.copy(self.full.at[owner], owner, p.sibling)
        for step in (0, 1, 3, 2):
            self.arrive(p.at(step, 1))

    def drain(self):
        for one in self.copies:
            one.wait_send()


class Exchange:
    def __init__(self, place, src, slots, send, recv, same=False):
        self.place, self.src, self.slots, self.send, self.recv = place, src, slots, send, recv
        self.copies = []
        self.same = same

    def block(self, t):
        return self.src if self.same else self.src.at[t]

    def start(self):
        p = self.place
        for k in range(1, p.nt):
            to = lax.rem(p.me + k, p.nt)
            one = remote(
                self.block(to),
                self.slots.at[p.me],
                self.send.at[k - 1],
                self.recv.at[p.me],
                {"tensor": to},
            )
            one.start()
            self.copies.append(one)
        self.slots[p.me] = self.block(p.me)[...]

    def finish(self):
        p = self.place
        for k in range(1, p.nt):
            owner = lax.rem(p.me + k, p.nt)
            remote(
                self.block(owner),
                self.slots.at[owner],
                self.send.at[0],
                self.recv.at[owner],
                {"tensor": owner},
            ).wait_recv()

    def drain(self):
        for one in self.copies:
            one.wait_send()


class PairReduce:
    def __init__(self, place, part, pair, joined, got, send, recv):
        self.place, self.part, self.pair, self.joined, self.got = place, part, pair, joined, got
        self.send, self.recv = send, recv
        self.copies = []

    def start(self, x):
        p = self.place
        one = remote(
            self.part.at[x * 2 + 1 - p.c],
            self.pair.at[x],
            self.send.at[x],
            self.recv.at[x],
            {"tensor": p.sibling},
        )
        one.start()
        self.copies.append(one)

    def join(self, x):
        p = self.place
        remote(
            self.part.at[x * 2 + p.c],
            self.pair.at[x],
            self.send.at[0],
            self.recv.at[x],
            {"tensor": p.sibling},
        ).wait_recv()
        return self.part[x * 2 + p.c].astype(F32) + self.pair[x].astype(F32)

    def middle(self):
        p = self.place
        nx = p.nx
        for i, step in enumerate((2, 1, 3)):
            x = lax.rem(p.x + step, nx)
            self.joined[i] = self.join(x).astype(BF16)
            one = remote(
                self.joined.at[i],
                self.got.at[p.x],
                self.send.at[nx + i],
                self.recv.at[nx + p.x],
                {"tensor": x * 2 + p.c},
            )
            one.start()
            self.copies.append(one)

    def finish(self):
        p = self.place
        nx = p.nx
        total = self.join(p.x)
        for i, step in enumerate((1, 3, 2)):
            x = lax.rem(p.x + step, nx)
            remote(
                self.joined.at[i],
                self.got.at[x],
                self.send.at[nx],
                self.recv.at[nx + x],
                {"tensor": x * 2 + p.c},
            ).wait_recv()
            total = total + self.got[x].astype(F32)
        return total

    def drain(self):
        for one in self.copies:
            one.wait_send()


class AllToAll:
    def __init__(self, count, src, slots, send, recv):
        self.count, self.src, self.slots, self.send, self.recv = count, src, slots, send, recv
        self.me = lax.axis_index("notes")

    def start(self):
        def step(j, carry):
            k = self.count // 2 + (j + 1) // 2 * (1 - 2 * lax.rem(j, 2))
            to = lax.rem(self.me + k, self.count)
            remote(
                self.src.at[to], self.slots.at[self.me], self.send, self.recv, {"notes": to}
            ).start()
            return carry

        lax.fori_loop(0, self.count - 1, step, 0)
        self.slots[self.me] = self.src[self.me]

    def finish(self):
        span = pl.ds(0, self.count - 1)
        remote(
            self.src.at[span], self.slots.at[span], self.send, self.recv, {"notes": self.me}
        ).wait()


def norm_rows(values, gain):
    centre = values - jnp.mean(values, axis=-1, keepdims=True)
    inverse = lax.rsqrt(jnp.mean(centre * centre, axis=-1, keepdims=True) + EPSILON)
    scaled = centre * inverse
    return scaled, inverse, (scaled * gain).astype(BF16)


def side_by_side(blocks):
    return jnp.concatenate([blocks[t] for t in range(blocks.shape[0])], axis=1)


def body(
    dims,
    pid,
    order,
    length,
    states_hbm,
    lq_hbm,
    pos_hbm,
    gain1_hbm,
    gain2_hbm,
    cot_hbm,
    outw_hbm,
    wv_hbm,
    qkv_hbm,
    up_hbm,
    down_hbm,
    visit_out,
    latent_out,
    value_out,
    query_out,
    states,
    lq,
    pos,
    gain1,
    gain2,
    cot,
    outw,
    wv,
    qkv,
    up,
    down,
    full,
    cotf,
    outf,
    codes_out,
    codes_in,
    probs,
    weights,
    values,
    mixture,
    slots,
    arrived,
    place_t,
    place,
    vloc,
    visitf,
    scaled1,
    inverse1,
    projected,
    vprobs,
    ctxl,
    ctxf,
    residual_own,
    scaled2,
    inverse2,
    hidden,
    hidden_grad,
    part2,
    pair2,
    joined2,
    got2,
    sum2,
    sum2f,
    context_grads,
    partf,
    pairf,
    joinedf,
    gotf,
    rgrad,
    part1,
    pair1,
    joined1,
    got1,
    stat,
    stats,
    slots2,
    arrived2,
    vpart,
    vgot,
    vpart2,
    vgot2,
    qpart,
    qgot,
    qpart2,
    qgot2,
    load_sem,
    ring_send,
    ring_recv,
    relay_send,
    relay_recv,
    ex_send,
    ex_recv,
    stat_send,
    stat_recv,
    a2a_send,
    a2a_recv,
    y_send,
    y_recv,
    z_send,
    z_recv,
):
    nn, ny, nt, notes, tok, lat, most = dims
    nz = nn // ny
    rows = most * lat
    width = 128
    tp = Place(nt)
    who = lax.axis_index("notes")
    wz, wy = who // ny, lax.rem(who, ny)

    loads = [
        pltpu.make_async_copy(src, dst, load_sem.at[i])
        for i, (src, dst) in enumerate(
            (
                (states_hbm, states),
                (lq_hbm, lq),
                (wv_hbm, wv),
                (pos_hbm, pos),
                (cot_hbm, cot),
                (outw_hbm, outw),
                (qkv_hbm.at[0], qkv.at[:, 0:width]),
                (qkv_hbm.at[1], qkv.at[:, width : 2 * width]),
                (qkv_hbm.at[2], qkv.at[:, 2 * width :]),
                (up_hbm, up),
                (down_hbm, down),
                (gain1_hbm, gain1),
                (gain2_hbm, gain2),
            )
        )
    ]
    barrier = pltpu.get_barrier_semaphore()

    def greet(j, carry):
        k = nn // 2 + (j + 1) // 2 * (1 - 2 * lax.rem(j, 2))
        pl.semaphore_signal(
            barrier, inc=1, device_id={"notes": lax.rem(who + k, nn)}, device_id_type=MESH
        )
        return carry

    lax.fori_loop(0, nn - 1, greet, 0)
    for k in range(1, nt):
        pl.semaphore_signal(
            barrier, inc=1, device_id={"tensor": lax.rem(tp.me + k, nt)}, device_id_type=MESH
        )
    for one in loads:
        one.start()
    pl.semaphore_wait(barrier, nt - 1 + nn - 1)

    ring_states = RingGather(tp, states, full, ring_send.at[0], ring_recv.at[0])
    ring_cot = RingGather(tp, cot, cotf, ring_send.at[1], ring_recv.at[1])
    ring_out = RingGather(tp, outw, outf, ring_send.at[2], ring_recv.at[2])
    loads[0].wait()
    ring_states.start()

    patient = iota((nn, 1, width), 0)
    codes = jnp.zeros((nn, 1, width), I32)
    for n in range(notes):
        codes = jnp.where(patient == pid[n], order[n] + 1, codes)
    codes_out[...] = codes
    route = AllToAll(nn, codes_out, codes_in, a2a_send.at[0], a2a_recv.at[0])

    loads[1].wait()
    low = (iota((1, width), 1) < HEAD).astype(F32)
    low_b, high_b = low.astype(BF16), (1.0 - low).astype(BF16)
    query = jnp.concatenate([lq[...] * low_b, lq[...] * high_b], axis=0)
    both = 2 * lat
    for n in range(notes):
        score = 0.125 * dot_nt(query, states[n * tok : (n + 1) * tok, :])
        score = jnp.exp(score - jnp.max(score, axis=-1, keepdims=True))
        prob = score / jnp.sum(score, axis=-1, keepdims=True)
        probs[n * both : (n + 1) * both, :] = prob
        weights[n * both : (n + 1) * both, :] = prob.astype(BF16)

    ring_states.pass_on()
    ring_states.relay_near()
    route.start()
    ring_states.relay_far()
    loads[4].wait()
    loads[5].wait()
    ring_cot.start()
    ring_out.start()
    ring_states.finish()

    loads[2].wait()
    pooled = []
    lane_low = iota((lat, width), 1) < HEAD
    for n in range(notes):
        here = pl.ds(n * tok, tok)
        note = jnp.concatenate([full[t, here, :] for t in range(nt)], axis=1)
        value = dot_nn(note, wv[...]).astype(BF16)
        values[here, :] = value
        mix = dot_nn(weights[n * both : (n + 1) * both, :], value)
        pooled.append(jnp.where(lane_low, mix[:lat], mix[lat:]))
    pooled = jnp.concatenate(pooled, axis=0).astype(BF16)

    line = iota((1, notes * lat), 1)
    target = lax.rem(line, lat)
    for n in range(notes):
        target = jnp.where(line // lat == n, target + pid[n] * lat, target)
    select = (iota((nn * lat, notes * lat), 0) == target).astype(F32).astype(BF16)
    slots[...] = dot_nn(select, pooled).astype(BF16).reshape(nn, lat, width)
    forward = AllToAll(nn, slots, arrived, a2a_send.at[1], a2a_recv.at[1])
    forward.start()

    ring_cot.pass_on()
    ring_out.pass_on()
    ring_cot.relay_near()
    ring_out.relay_near()
    ring_cot.relay_far()
    ring_out.relay_far()

    route.finish()
    code = jnp.broadcast_to(codes_in[...], (nn, lat, width)).reshape(nn * lat, width)
    slot_row = jnp.where(code > 0, (code - 1) * lat + lax.rem(iota((nn * lat, width), 0), lat), -1)
    padded = place_t.shape[1]
    placing = jnp.concatenate(
        [
            (iota((nn * lat, width), 1) + j * width == slot_row).astype(F32)
            for j in range(padded // width)
        ],
        axis=1,
    )
    place_t[...] = placing.astype(BF16)
    place[...] = jnp.transpose(placing).astype(BF16)

    for n in range(notes):
        here = pl.ds(n * tok, tok)
        note = jnp.concatenate([full[t, here, :] for t in range(nt)], axis=1)
        mixed = dot_nn(weights[n * both : (n + 1) * both, :], note)
        mixture[n * both : (n + 1) * both, :] = mixed.astype(BF16)

    loads[3].wait()
    limit = length[0] * lat
    row_valid = iota((rows, width), 0) < limit
    positions = pos[...].astype(F32)
    positions = jnp.concatenate(
        [jnp.broadcast_to(positions[m : m + 1, :], (lat, width)) for m in range(most)], axis=0
    )
    ring_cot.finish()
    ring_out.finish()
    for one in loads[6:]:
        one.wait()
    out_grad = jnp.where(iota((rows, nt * width), 0) < limit, side_by_side(cotf).astype(F32), 0.0)
    hidden_grad[...] = dot_nt(out_grad.astype(BF16), down[...])

    forward.finish()
    placed = dot_nn(place[...], arrived[...].reshape(nn * lat, width))[:rows]
    vloc[...] = jnp.where(row_valid, placed + positions, 0.0).astype(BF16)

    half = rows // 2
    spans = [slice(j * half, (j + 1) * half) for j in range(2)]

    def relays(src, whole, k):
        return [
            RelayGather(
                tp,
                src.at[pl.ds(j * half, half)],
                whole.at[j],
                relay_send.at[k, j],
                relay_recv.at[k, j],
            )
            for j in range(2)
        ]

    gathers1 = relays(vloc, visitf, 0)
    for gather in gathers1:
        gather.start()
    for span, gather, blocks in zip(spans, gathers1, (visitf.at[0], visitf.at[1])):
        gather.finish()
        scaled, inverse, normed = norm_rows(side_by_side(blocks).astype(F32), gain1[...])
        scaled1[span, :] = scaled
        inverse1[span, :] = jnp.broadcast_to(inverse, (half, width))
        projected[span, :] = dot_nn(normed, qkv[...]).astype(BF16)
    q, k, v = (projected[:, j * width : (j + 1) * width] for j in range(3))
    key_valid = iota((1, rows), 1) < limit
    gathers2 = relays(ctxl, ctxf, 1)
    half_low = iota((half, width), 1) < HEAD
    key_heads = (k * low_b, k * high_b)
    for span, gather in zip(spans, gathers2):
        contexts = []
        for h in range(2):
            score = jnp.where(key_valid, 0.125 * dot_nt(q[span], key_heads[h]), MASKED)
            score = jnp.exp(score - jnp.max(score, axis=-1, keepdims=True))
            prob = score / jnp.sum(score, axis=-1, keepdims=True)
            vprobs[h, span, :] = prob
            contexts.append(dot_nn(prob.astype(BF16), v))
        ctxl[span, :] = jnp.where(half_low, contexts[0], contexts[1]).astype(BF16)
        gather.start()

    reduces2 = [
        PairReduce(
            tp, part2.at[j], pair2.at[j], joined2.at[j], got2.at[j], ex_send.at[j], ex_recv.at[j]
        )
        for j in range(2)
    ]
    own = pl.ds(pl.multiple_of(tp.me * width, width), width)
    for j, span in enumerate(spans):
        gathers2[j].finish()
        attention = dot_nn(side_by_side(ctxf.at[j]), outf[...].reshape(nt * width, nt * width))
        residual = side_by_side(visitf.at[j]).astype(F32) + attention
        scaled, inverse, normed = norm_rows(residual, gain2[...])
        rgrad[span, :] = residual
        scaled2[span, :] = scaled
        inverse2[span, :] = jnp.broadcast_to(inverse, (half, width))
        upper = dot_nn(normed, up[...])
        if j:
            reduces2[0].middle()
        bend = jnp.tanh(0.7978845608028654 * (upper + 0.044715 * upper * upper * upper))
        hidden[span, :] = (0.5 * upper * (1.0 + bend)).astype(BF16)
        slope = 0.5 * (1.0 + bend) + 0.5 * upper * (1.0 - bend * bend) * (
            0.7978845608028654 * (1.0 + 3.0 * 0.044715 * upper * upper)
        )
        upper_grad = (hidden_grad[span, :] * slope).astype(BF16)
        for x in range(nt // 2):
            pair = dot_nt(upper_grad, up[2 * x * width : 2 * (x + 1) * width, :]).astype(BF16)
            part2[j, 2 * x] = pair[:, :width]
            part2[j, 2 * x + 1] = pair[:, width:]
            reduces2[j].start(x)
    reduces2[1].middle()
    residual_own[...] = rgrad[:, own]
    gathers3 = relays(sum2, sum2f, 2)
    for span, reduce, gather in zip(spans, reduces2, gathers3):
        sum2[span, :] = reduce.finish().astype(BF16)
        gather.start()
    for j, span in enumerate(spans):
        gathers3[j].finish()
        weighted = side_by_side(sum2f.at[j]).astype(F32) * gain2[...]
        centred = weighted - jnp.mean(weighted, axis=-1, keepdims=True)
        given = jnp.concatenate([cotf[t, span, :] for t in range(nt)], axis=1).astype(F32)
        row = iota((half, nt * width), 0) + j * half
        scaled = scaled2[span, :]
        residual_grad = jnp.where(row < limit, given, 0.0) + inverse2[span, 0:1] * (
            centred - scaled * jnp.mean(weighted * scaled, axis=-1, keepdims=True)
        )
        rgrad[span, :] = residual_grad
        context_grads[span, :] = dot_nt(residual_grad.astype(BF16), outw[...]).astype(BF16)

    q, k, v = (projected[:, j * width : (j + 1) * width] for j in range(3))
    context_grad = context_grads[...]
    row_low = iota((rows, width), 1) < HEAD
    query_grads, key_grads, value_grads = [], [], []
    for h, mask in enumerate((low_b, high_b)):
        prob = vprobs[h]
        weight_grad = dot_nt(context_grad, v * mask)
        value_grads.append(dot_tn(prob.astype(BF16), context_grad))
        score_grad = (
            0.125 * prob * (weight_grad - jnp.sum(weight_grad * prob, axis=-1, keepdims=True))
        ).astype(BF16)
        query_grads.append(dot_nn(score_grad, k))
        key_grads.append(dot_tn(score_grad, q))
    packed = jnp.concatenate(
        [
            jnp.where(row_low, pair[0], pair[1]).astype(BF16)
            for pair in (query_grads, key_grads, value_grads)
        ],
        axis=1,
    )
    first_sum = jnp.zeros((rows, 1), F32)
    second_sum = jnp.zeros((rows, 1), F32)
    reduce1 = PairReduce(tp, part1, pair1, joined1, got1, ex_send.at[2], ex_recv.at[2])
    for x in range(nt // 2):
        cols = slice(2 * x * width, 2 * (x + 1) * width)
        partial = dot_nt(packed, qkv[cols, :])
        part1[2 * x] = partial[:, :width].astype(BF16)
        part1[2 * x + 1] = partial[:, width:].astype(BF16)
        reduce1.start(x)
        weighted = partial * gain1[:, cols]
        first_sum = first_sum + jnp.sum(weighted, axis=-1, keepdims=True)
        second_sum = second_sum + jnp.sum(weighted * scaled1[:, cols], axis=-1, keepdims=True)
    reduce1.middle()
    lane = iota((rows, width), 1)
    both_sums = jnp.where(lane == 0, first_sum, jnp.where(lane == 1, second_sum, 0.0))
    stat[...] = jnp.transpose(
        jnp.concatenate([both_sums, jnp.zeros((padded - rows, width), F32)], axis=0)
    )[:8]
    gather4 = Exchange(tp, stat, stats, stat_send, stat_recv, same=True)
    gather4.start()
    total = reduce1.finish()
    gather4.finish()
    means = stats[0]
    for t in range(1, nt):
        means = means + stats[t]
    means = jnp.transpose(
        jnp.concatenate([means, jnp.zeros((width - 8, padded), F32)], axis=0)
    )[:rows] * (1.0 / (nt * width))
    visit_grad = rgrad[:, own] + inverse1[...] * (
        total * gain1[:, own] - means[:, 0:1] - scaled1[:, own] * means[:, 1:2]
    )
    visit_grad = visit_grad.astype(BF16)
    slots2[...] = dot_nn(place_t[:, :rows], visit_grad).astype(BF16).reshape(nn, lat, width)
    back = AllToAll(nn, slots2, arrived2, a2a_send.at[2], a2a_recv.at[2])
    back.start()

    reducef = PairReduce(tp, partf, pairf, joinedf, gotf, ex_send.at[3], ex_recv.at[3])
    for x in range(nt // 2):
        pair = dot_nn(hidden[...], down[:, 2 * x * width : 2 * (x + 1) * width]).astype(BF16)
        partf[2 * x] = pair[:, :width]
        partf[2 * x + 1] = pair[:, width:]
        reducef.start(x)
    reducef.middle()
    column = iota((notes * lat, 1), 0)
    wanted = lax.rem(column, lat)
    for n in range(notes):
        wanted = jnp.where(column // lat == n, wanted + pid[n] * lat, wanted)
    unselect = (iota((notes * lat, nn * lat), 1) == wanted).astype(F32).astype(BF16)
    total = reducef.finish()
    visit_out[...] = jnp.where(row_valid, residual_own[...] + total, 0.0).astype(BF16)
    for one in gathers1 + gathers2 + gathers3 + reduces2 + [reduce1, reducef, gather4]:
        one.drain()

    back.finish()
    latent = dot_nn(unselect, arrived2[...].reshape(nn * lat, width)).astype(BF16)
    latent_out[...] = latent
    halves = (latent * low_b, latent * high_b)
    spread = jnp.concatenate(
        [half[n * lat : (n + 1) * lat] for n in range(notes) for half in halves], axis=0
    )
    partial = dot_tn(mixture[...], spread).astype(BF16)
    vpart[...] = partial.reshape(nz, ny, lat, width)
    query_total = jnp.zeros((both, width), F32)
    for n in range(notes):
        here = slice(n * both, (n + 1) * both)
        tokens = slice(n * tok, (n + 1) * tok)
        prob = probs[here, :]
        prob_grad = dot_nt(spread[here], values[tokens, :])
        score_grad = prob * (prob_grad - jnp.sum(prob_grad * prob, axis=-1, keepdims=True))
        query_total = query_total + dot_nn(score_grad.astype(BF16), states[tokens, :])
    qpart[...] = 0.125 * jnp.where(lane_low, query_total[:lat], query_total[lat:])

    y_copies = []
    for s in range(1, ny):
        to = lax.rem(wy + s, ny)
        device = {"notes": wz * ny + to}
        for i, (src, dst) in enumerate(((vpart.at[:, to], vgot.at[wy]), (qpart, qgot.at[wy]))):
            one = remote(src, dst, y_send.at[i, s], y_recv.at[i, wy], device)
            one.start()
            y_copies.append(one)
    total = vpart[:, wy].astype(F32)
    query_sum = qpart[...]
    for s in range(1, ny):
        owner = lax.rem(wy + s, ny)
        device = {"notes": wz * ny + owner}
        for i, (src, dst) in enumerate(((vpart.at[:, owner], vgot.at[owner]), (qpart, qgot.at[owner]))):
            remote(src, dst, y_send.at[i, s], y_recv.at[i, owner], device).wait_recv()
        total = total + vgot[owner].astype(F32)
        query_sum = query_sum + qgot[owner]
    vpart2[...] = total.astype(BF16)
    qpart2[...] = query_sum.astype(BF16)

    def along_z(j, carry):
        to = lax.rem(wz + nz // 2 + (j + 1) // 2 * (1 - 2 * lax.rem(j, 2)), nz)
        device = {"notes": to * ny + wy}
        remote(vpart2.at[to], vgot2.at[wz], z_send.at[0], z_recv.at[0], device).start()
        remote(qpart2, qgot2.at[wz], z_send.at[1], z_recv.at[1], device).start()
        return carry

    lax.fori_loop(0, nz - 1, along_z, 0)
    vgot2[wz] = vpart2[wz]
    qgot2[wz] = qpart2[...]
    for one in y_copies:
        one.wait_send()
    span = pl.ds(0, nz - 1)
    remote(vpart2.at[span], vgot2.at[span], z_send.at[0], z_recv.at[0], {"notes": who}).wait()
    remote(qgot2.at[span], qgot2.at[span], z_send.at[1], z_recv.at[1], {"notes": who}).wait()
    total = vgot2[0].astype(F32)
    query_sum = qgot2[0].astype(F32)
    for z in range(1, nz):
        total = total + vgot2[z].astype(F32)
        query_sum = query_sum + qgot2[z].astype(F32)
    value_out[...] = total
    query_out[...] = query_sum


def hand_over(a, b, c, d, a_out, b_out, c_out, d_out):
    for src, dst in ((a, a_out), (b, b_out), (c, c_out), (d, d_out)):
        dst[...] = src[...]


def shards(
    mesh_shape,
    states,
    value_weight,
    latent_query,
    patient_ids,
    note_order,
    history_length,
    position_table,
    attention_gain,
    feedforward_gain,
    qkv_weight,
    out_weight,
    up_weight,
    down_weight,
    cotangent,
):
    nn, nt = mesh_shape["notes"], mesh_shape["tensor"]
    ny = 4
    nz = nn // ny
    notes, tok, width = states.shape
    lat, most = latent_query.shape[0], position_table.shape[0]
    rows = most * lat
    dim = nt * width
    inner = up_weight.shape[1]
    padded = -(-rows // 128) * 128
    both = 2 * lat
    dims = (nn, ny, nt, notes, tok, lat, most)
    vmem = pl.BlockSpec(memory_space=pltpu.VMEM)
    smem = pl.BlockSpec(memory_space=pltpu.SMEM)
    hbm = pl.BlockSpec(memory_space=pl.ANY)
    V = pltpu.VMEM
    dma = pltpu.SemaphoreType.DMA
    block = (nt, rows, width)
    halves = (2, nt, rows // 2, width)
    nx = nt // 2
    scratch = [
        V((notes * tok, width), BF16),
        V((lat, width), BF16),
        V((most, width), BF16),
        V((1, dim), F32),
        V((1, dim), F32),
        V((rows, width), BF16),
        V((width, dim), BF16),
        V((dim, width), BF16),
        V((dim, 3 * width), BF16),
        V((dim, inner), BF16),
        V((inner, dim), BF16),
        V((nt, notes * tok, width), BF16),
        V(block, BF16),
        V((nt, width, dim), BF16),
        V((nn, 1, width), I32),
        V((nn, 1, width), I32),
        V((notes * both, tok), F32),
        V((notes * both, tok), BF16),
        V((notes * tok, width), BF16),
        V((notes * both, dim), BF16),
        V((nn, lat, width), BF16),
        V((nn, lat, width), BF16),
        V((nn * lat, padded), BF16),
        V((padded, nn * lat), BF16),
        V((rows, width), BF16),
        V(halves, BF16),
        V((rows, dim), F32),
        V((rows, width), F32),
        V((rows, 3 * width), BF16),
        V((2, rows, rows), F32),
        V((rows, width), BF16),
        V(halves, BF16),
        V((rows, width), F32),
        V((rows, dim), F32),
        V((rows, width), F32),
        V((rows, inner), BF16),
        V((rows, inner), F32),
        V(halves, BF16),
        V((2, nx, rows // 2, width), BF16),
        V((2, nx - 1, rows // 2, width), BF16),
        V((2, nx, rows // 2, width), BF16),
        V((rows, width), BF16),
        V(halves, BF16),
        V((rows, width), BF16),
        V(block, BF16),
        V((nx, rows, width), BF16),
        V((nx - 1, rows, width), BF16),
        V((nx, rows, width), BF16),
        V((rows, dim), F32),
        V(block, BF16),
        V((nx, rows, width), BF16),
        V((nx - 1, rows, width), BF16),
        V((nx, rows, width), BF16),
        V((8, padded), F32),
        V((nt, 8, padded), F32),
        V((nn, lat, width), BF16),
        V((nn, lat, width), BF16),
        V((nz, ny, lat, width), BF16),
        V((ny, nz, lat, width), BF16),
        V((nz, lat, width), BF16),
        V((nz, lat, width), BF16),
        V((lat, width), F32),
        V((ny, lat, width), F32),
        V((lat, width), BF16),
        V((nz, lat, width), BF16),
        dma((13,)),
        dma((3, 14)),
        dma((3, nt, 2)),
        dma((3, 2, 7)),
        dma((3, 2, nt)),
        dma((4, nt - 1)),
        dma((4, nt)),
        dma((nt - 1,)),
        dma((nt,)),
        dma((3,)),
        dma((3,)),
        dma((2, ny)),
        dma((2, ny)),
        dma((2,)),
        dma((2,)),
    ]
    visit_out, latent_grads, value_grad, query_grad = pl.pallas_call(
        functools.partial(body, dims),
        out_shape=(
            jax.ShapeDtypeStruct((rows, width), BF16),
            jax.ShapeDtypeStruct((notes * lat, width), BF16),
            jax.ShapeDtypeStruct((dim // nn, width), F32),
            jax.ShapeDtypeStruct((lat, width), F32),
        ),
        in_specs=[smem] * 3 + [hbm] * 11,
        out_specs=(vmem,) * 4,
        scratch_shapes=scratch,
        name="note_visit_step",
        compiler_params=pltpu.CompilerParams(
            collective_id=0, has_side_effects=True, vmem_limit_bytes=56 * 2**20
        ),
    )(
        patient_ids,
        note_order,
        history_length,
        states.reshape(notes * tok, width),
        latent_query,
        position_table,
        attention_gain.reshape(1, dim),
        feedforward_gain.reshape(1, dim),
        cotangent.reshape(rows, width),
        out_weight,
        value_weight,
        jnp.transpose(qkv_weight, (1, 0, 2)),
        up_weight,
        down_weight,
    )
    results = (visit_out, latent_grads, value_grad, query_grad)
    visit_out, latent_grads, value_grad, query_grad = pl.pallas_call(
        hand_over,
        out_shape=tuple(jax.ShapeDtypeStruct(r.shape, r.dtype) for r in results),
        in_specs=[vmem] * 4,
        out_specs=(vmem,) * 4,
        name="hand_over",
    )(*results)
    return (
        visit_out[None],
        latent_grads.reshape(notes, lat, width),
        value_grad,
        query_grad,
    )


def solution(mesh):
    return jax.shard_map(
        functools.partial(shards, dict(mesh.shape)),
        mesh=mesh,
        in_specs=(
            P("notes", None, "tensor"),
            P(None, "tensor"),
            P(None, "tensor"),
            P("notes"),
            P("notes"),
            P("notes"),
            P(None, "tensor"),
            P(),
            P(),
            P(None, None, "tensor"),
            P("tensor", None),
            P(None, "tensor"),
            P("tensor", None),
            P("notes", None, "tensor"),
        ),
        out_specs=(
            P("notes", None, "tensor"),
            P("notes", None, "tensor"),
            P("notes", "tensor"),
            P(None, "tensor"),
        ),
        check_vma=False,
    )
```

```python
import functools

import jax
import jax.numpy as jnp
from jax import lax
from jax.experimental import pallas as pl
from jax.experimental.pallas import tpu as pltpu
from jax.sharding import PartitionSpec as P

HEAD = 64
EPSILON = 1e-05
MASKED = -1e30
MESH = pl.DeviceIdType.MESH
F32 = jnp.float32
BF16 = jnp.bfloat16
I32 = jnp.int32


def remote(src, dst, send, recv, device):
    return pltpu.make_async_remote_copy(
        src_ref=src,
        dst_ref=dst,
        send_sem=send,
        recv_sem=recv,
        device_id=device,
        device_id_type=MESH,
    )


def dot_nn(a, b):
    return lax.dot_general(a, b, (((1,), (0,)), ((), ())), preferred_element_type=F32)


def dot_nt(a, b):
    return lax.dot_general(a, b, (((1,), (1,)), ((), ())), preferred_element_type=F32)


def dot_tn(a, b):
    return lax.dot_general(a, b, (((0,), (0,)), ((), ())), preferred_element_type=F32)


def iota(shape, dim):
    return lax.broadcasted_iota(I32, shape, dim)


class Place:
    def __init__(self, nt):
        self.nt = nt
        self.nx = nt // 2
        self.me = lax.axis_index("tensor")
        self.x = self.me // 2
        self.c = lax.rem(self.me, 2)
        self.sibling = self.at(0, 1)

    def at(self, step, flip):
        core = 1 - self.c if flip else self.c
        return lax.rem(self.x + step, self.nx) * 2 + core


class RingGather:
    def __init__(self, place, src, full, send, recv):
        self.place, self.src, self.full, self.send, self.recv = place, src, full, send, recv
        self.half = src.shape[0] // 2
        self.copies = []

    def part(self, ref, j):
        return ref.at[pl.ds(j * self.half, self.half)]

    def copy(self, src, owner, j, to):
        one = remote(
            src,
            self.part(self.full.at[owner], j),
            self.send.at[len(self.copies)],
            self.recv.at[owner, j],
            {"tensor": to},
        )
        one.start()
        self.copies.append(one)

    def arrive(self, owner, j):
        remote(
            self.part(self.src, j),
            self.part(self.full.at[owner], j),
            self.send.at[0],
            self.recv.at[owner, j],
            {"tensor": owner},
        ).wait_recv()

    def start(self):
        p = self.place
        right, left = p.at(1, 0), p.at(3, 0)
        for j, to in ((0, right), (1, left), (0, p.sibling), (1, p.sibling)):
            self.copy(self.part(self.src, j), p.me, j, to)
        self.full[p.me] = self.src[...]

    def second(self):
        p = self.place
        for one in self.copies[:2]:
            one.wait_send()
        for j, to in ((1, p.at(1, 0)), (0, p.at(3, 0))):
            self.copy(self.part(self.src, j), p.me, j, to)

    def pass_on(self):
        p = self.place
        right, left = p.at(1, 0), p.at(3, 0)
        for owner, j, to in ((left, 0, right), (right, 1, left)):
            self.arrive(owner, j)
            self.copy(self.part(self.full.at[owner], j), owner, j, to)
            self.copy(self.part(self.full.at[owner], j), owner, j, p.sibling)

    def relay_near(self):
        p = self.place
        for owner, j in ((p.at(3, 0), 1), (p.at(1, 0), 0)):
            self.arrive(owner, j)
            self.copy(self.part(self.full.at[owner], j), owner, j, p.sibling)

    def relay_far(self):
        p = self.place
        for j in range(2):
            self.arrive(p.at(2, 0), j)
            self.copy(self.part(self.full.at[p.at(2, 0)], j), p.at(2, 0), j, p.sibling)

    def finish(self):
        for step in (0, 1, 3, 2):
            for j in range(2):
                self.arrive(self.place.at(step, 1), j)
        for one in self.copies[2:]:
            one.wait_send()


class RelayGather:
    def __init__(self, place, src, full, send, recv):
        self.place, self.src, self.full, self.send, self.recv = place, src, full, send, recv
        self.copies = []

    def copy(self, src, owner, to):
        one = remote(
            src,
            self.full.at[owner],
            self.send.at[len(self.copies)],
            self.recv.at[owner],
            {"tensor": to},
        )
        one.start()
        self.copies.append(one)

    def arrive(self, owner):
        remote(
            self.src, self.full.at[owner], self.send.at[0], self.recv.at[owner], {"tensor": owner}
        ).wait_recv()

    def start(self):
        p = self.place
        for to in (p.at(2, 0), p.at(1, 0), p.at(3, 0), p.sibling):
            self.copy(self.src, p.me, to)
        self.full[p.me] = self.src[...]

    def finish(self):
        p = self.place
        for step in (1, 3, 2):
            owner = p.at(step, 0)
            self.arrive(owner)
            self.copy(self.full.at[owner], owner, p.sibling)
        for step in (0, 1, 3, 2):
            self.arrive(p.at(step, 1))

    def drain(self):
        for one in self.copies:
            one.wait_send()


class Exchange:
    def __init__(self, place, src, slots, send, recv, same=False):
        self.place, self.src, self.slots, self.send, self.recv = place, src, slots, send, recv
        self.copies = []
        self.same = same

    def block(self, t):
        return self.src if self.same else self.src.at[t]

    def start(self):
        p = self.place
        for k in range(1, p.nt):
            to = lax.rem(p.me + k, p.nt)
            one = remote(
                self.block(to),
                self.slots.at[p.me],
                self.send.at[k - 1],
                self.recv.at[p.me],
                {"tensor": to},
            )
            one.start()
            self.copies.append(one)
        self.slots[p.me] = self.block(p.me)[...]

    def finish(self):
        p = self.place
        for k in range(1, p.nt):
            owner = lax.rem(p.me + k, p.nt)
            remote(
                self.block(owner),
                self.slots.at[owner],
                self.send.at[0],
                self.recv.at[owner],
                {"tensor": owner},
            ).wait_recv()

    def drain(self):
        for one in self.copies:
            one.wait_send()


class PairReduce:
    def __init__(self, place, part, pair, joined, got, send, recv):
        self.place, self.part, self.pair, self.joined, self.got = place, part, pair, joined, got
        self.send, self.recv = send, recv
        self.copies = []

    def start(self, x):
        p = self.place
        one = remote(
            self.part.at[x * 2 + 1 - p.c],
            self.pair.at[x],
            self.send.at[x],
            self.recv.at[x],
            {"tensor": p.sibling},
        )
        one.start()
        self.copies.append(one)

    def join(self, x):
        p = self.place
        remote(
            self.part.at[x * 2 + p.c],
            self.pair.at[x],
            self.send.at[0],
            self.recv.at[x],
            {"tensor": p.sibling},
        ).wait_recv()
        return self.part[x * 2 + p.c].astype(F32) + self.pair[x].astype(F32)

    def middle(self):
        p = self.place
        nx = p.nx
        for i, step in enumerate((2, 1, 3)):
            x = lax.rem(p.x + step, nx)
            self.joined[i] = self.join(x).astype(BF16)
            one = remote(
                self.joined.at[i],
                self.got.at[p.x],
                self.send.at[nx + i],
                self.recv.at[nx + p.x],
                {"tensor": x * 2 + p.c},
            )
            one.start()
            self.copies.append(one)

    def finish(self):
        p = self.place
        nx = p.nx
        total = self.join(p.x)
        for i, step in enumerate((1, 3, 2)):
            x = lax.rem(p.x + step, nx)
            remote(
                self.joined.at[i],
                self.got.at[x],
                self.send.at[nx],
                self.recv.at[nx + x],
                {"tensor": x * 2 + p.c},
            ).wait_recv()
            total = total + self.got[x].astype(F32)
        return total

    def drain(self):
        for one in self.copies:
            one.wait_send()


class AllToAll:
    def __init__(self, count, src, slots, send, recv):
        self.count, self.src, self.slots, self.send, self.recv = count, src, slots, send, recv
        self.me = lax.axis_index("notes")

    def start(self):
        def step(j, carry):
            k = self.count // 2 + (j + 1) // 2 * (1 - 2 * lax.rem(j, 2))
            to = lax.rem(self.me + k, self.count)
            remote(
                self.src.at[to], self.slots.at[self.me], self.send, self.recv, {"notes": to}
            ).start()
            return carry

        lax.fori_loop(0, self.count - 1, step, 0)
        self.slots[self.me] = self.src[self.me]

    def finish(self):
        span = pl.ds(0, self.count - 1)
        remote(
            self.src.at[span], self.slots.at[span], self.send, self.recv, {"notes": self.me}
        ).wait()


def norm_rows(values, gain):
    centre = values - jnp.mean(values, axis=-1, keepdims=True)
    inverse = lax.rsqrt(jnp.mean(centre * centre, axis=-1, keepdims=True) + EPSILON)
    scaled = centre * inverse
    return scaled, inverse, (scaled * gain).astype(BF16)


def side_by_side(blocks):
    return jnp.concatenate([blocks[t] for t in range(blocks.shape[0])], axis=1)


def body(
    dims,
    pid,
    order,
    length,
    states_hbm,
    lq_hbm,
    pos_hbm,
    gain1_hbm,
    gain2_hbm,
    cot_hbm,
    outw_hbm,
    wv_hbm,
    qkv_hbm,
    up_hbm,
    down_hbm,
    visit_out,
    latent_out,
    value_out,
    query_out,
    states,
    lq,
    pos,
    gain1,
    gain2,
    cot,
    outw,
    wv,
    qkv,
    up,
    down,
    full,
    cotf,
    outf,
    codes_out,
    codes_in,
    probs,
    weights,
    values,
    mixture,
    slots,
    arrived,
    place_t,
    place,
    vloc,
    visitf,
    scaled1,
    inverse1,
    projected,
    vprobs,
    ctxl,
    ctxf,
    residual_own,
    scaled2,
    inverse2,
    hidden,
    hidden_grad,
    part2,
    pair2,
    joined2,
    got2,
    sum2,
    sum2f,
    context_grads,
    partf,
    pairf,
    joinedf,
    gotf,
    rgrad,
    part1,
    pair1,
    joined1,
    got1,
    stat,
    stats,
    slots2,
    arrived2,
    vpart,
    vgot,
    vpart2,
    vgot2,
    qpart,
    qgot,
    qpart2,
    qgot2,
    load_sem,
    ring_send,
    ring_recv,
    relay_send,
    relay_recv,
    ex_send,
    ex_recv,
    stat_send,
    stat_recv,
    a2a_send,
    a2a_recv,
    y_send,
    y_recv,
    z_send,
    z_recv,
):
    nn, ny, nt, notes, tok, lat, most = dims
    nz = nn // ny
    rows = most * lat
    width = 128
    tp = Place(nt)
    who = lax.axis_index("notes")
    wz, wy = who // ny, lax.rem(who, ny)

    loads = [
        pltpu.make_async_copy(src, dst, load_sem.at[i])
        for i, (src, dst) in enumerate(
            (
                (states_hbm, states),
                (lq_hbm, lq),
                (wv_hbm, wv),
                (pos_hbm, pos),
                (cot_hbm, cot),
                (outw_hbm, outw),
                (qkv_hbm.at[0], qkv.at[:, 0:width]),
                (qkv_hbm.at[1], qkv.at[:, width : 2 * width]),
                (qkv_hbm.at[2], qkv.at[:, 2 * width :]),
                (up_hbm, up),
                (down_hbm, down),
                (gain1_hbm, gain1),
                (gain2_hbm, gain2),
            )
        )
    ]
    barrier = pltpu.get_barrier_semaphore()

    def greet(j, carry):
        k = nn // 2 + (j + 1) // 2 * (1 - 2 * lax.rem(j, 2))
        pl.semaphore_signal(
            barrier, inc=1, device_id={"notes": lax.rem(who + k, nn)}, device_id_type=MESH
        )
        return carry

    lax.fori_loop(0, nn - 1, greet, 0)
    for k in range(1, nt):
        pl.semaphore_signal(
            barrier, inc=1, device_id={"tensor": lax.rem(tp.me + k, nt)}, device_id_type=MESH
        )
    for one in loads[:2]:
        one.start()
    pl.semaphore_wait(barrier, nt - 1 + nn - 1)

    ring_states = RingGather(tp, states, full, ring_send.at[0], ring_recv.at[0])
    ring_cot = RingGather(tp, cot, cotf, ring_send.at[1], ring_recv.at[1])
    ring_out = RingGather(tp, outw, outf, ring_send.at[2], ring_recv.at[2])
    loads[0].wait()
    ring_states.start()
    for one in loads[2:]:
        one.start()

    patient = iota((nn, 1, width), 0)
    codes = jnp.zeros((nn, 1, width), I32)
    for n in range(notes):
        codes = jnp.where(patient == pid[n], order[n] + 1, codes)
    codes_out[...] = codes
    route = AllToAll(nn, codes_out, codes_in, a2a_send.at[0], a2a_recv.at[0])

    loads[1].wait()
    low = (iota((1, width), 1) < HEAD).astype(F32)
    low_b, high_b = low.astype(BF16), (1.0 - low).astype(BF16)
    query = jnp.concatenate([lq[...] * low_b, lq[...] * high_b], axis=0)
    both = 2 * lat
    for n in range(notes):
        score = 0.125 * dot_nt(query, states[n * tok : (n + 1) * tok, :])
        score = jnp.exp(score - jnp.max(score, axis=-1, keepdims=True))
        prob = score / jnp.sum(score, axis=-1, keepdims=True)
        probs[n * both : (n + 1) * both, :] = prob
        weights[n * both : (n + 1) * both, :] = prob.astype(BF16)

    ring_states.second()
    ring_states.pass_on()
    ring_states.relay_near()
    route.start()
    ring_states.relay_far()
    loads[4].wait()
    loads[5].wait()
    ring_cot.start()
    ring_out.start()
    ring_cot.second()
    ring_out.second()
    ring_states.finish()

    loads[2].wait()
    pooled = []
    lane_low = iota((lat, width), 1) < HEAD
    for n in range(notes):
        here = pl.ds(n * tok, tok)
        note = jnp.concatenate([full[t, here, :] for t in range(nt)], axis=1)
        value = dot_nn(note, wv[...]).astype(BF16)
        values[here, :] = value
        mix = dot_nn(weights[n * both : (n + 1) * both, :], value)
        pooled.append(jnp.where(lane_low, mix[:lat], mix[lat:]))
    pooled = jnp.concatenate(pooled, axis=0).astype(BF16)

    line = iota((1, notes * lat), 1)
    target = lax.rem(line, lat)
    for n in range(notes):
        target = jnp.where(line // lat == n, target + pid[n] * lat, target)
    select = (iota((nn * lat, notes * lat), 0) == target).astype(F32).astype(BF16)
    slots[...] = dot_nn(select, pooled).astype(BF16).reshape(nn, lat, width)
    forward = AllToAll(nn, slots, arrived, a2a_send.at[1], a2a_recv.at[1])
    forward.start()

    ring_cot.pass_on()
    ring_out.pass_on()
    ring_cot.relay_near()
    ring_out.relay_near()
    ring_cot.relay_far()
    ring_out.relay_far()

    route.finish()
    code = jnp.broadcast_to(codes_in[...], (nn, lat, width)).reshape(nn * lat, width)
    slot_row = jnp.where(code > 0, (code - 1) * lat + lax.rem(iota((nn * lat, width), 0), lat), -1)
    padded = place_t.shape[1]
    placing = jnp.concatenate(
        [
            (iota((nn * lat, width), 1) + j * width == slot_row).astype(F32)
            for j in range(padded // width)
        ],
        axis=1,
    )
    place_t[...] = placing.astype(BF16)
    place[...] = jnp.transpose(placing).astype(BF16)

    mixed = []
    for n in range(notes):
        here = pl.ds(n * tok, tok)
        note = jnp.concatenate([full[t, here, :] for t in range(nt)], axis=1)
        mixed.append(dot_nn(weights[n * both : (n + 1) * both, :], note))
    mixture[...] = jnp.transpose(jnp.concatenate(mixed, axis=0)).astype(BF16)

    loads[3].wait()
    limit = length[0] * lat
    row_valid = iota((rows, width), 0) < limit
    positions = pos[...].astype(F32)
    positions = jnp.concatenate(
        [jnp.broadcast_to(positions[m : m + 1, :], (lat, width)) for m in range(most)], axis=0
    )
    ring_cot.finish()
    ring_out.finish()
    for one in loads[6:]:
        one.wait()
    out_grad = jnp.where(iota((rows, nt * width), 0) < limit, side_by_side(cotf).astype(F32), 0.0)
    hidden_grad[...] = dot_nt(out_grad.astype(BF16), down[...])

    forward.finish()
    placed = dot_nn(place[...], arrived[...].reshape(nn * lat, width))[:rows]
    vloc[...] = jnp.where(row_valid, placed + positions, 0.0).astype(BF16)

    half = rows // 2
    spans = [slice(j * half, (j + 1) * half) for j in range(2)]

    def relays(src, whole, k):
        return [
            RelayGather(
                tp,
                src.at[pl.ds(j * half, half)],
                whole.at[j],
                relay_send.at[k, j],
                relay_recv.at[k, j],
            )
            for j in range(2)
        ]

    gathers1 = relays(vloc, visitf, 0)
    for gather in gathers1:
        gather.start()
    for span, gather, blocks in zip(spans, gathers1, (visitf.at[0], visitf.at[1])):
        gather.finish()
        scaled, inverse, normed = norm_rows(side_by_side(blocks).astype(F32), gain1[...])
        scaled1[span, :] = scaled
        inverse1[span, :] = jnp.broadcast_to(inverse, (half, width))
        projected[span, :] = dot_nn(normed, qkv[...]).astype(BF16)
    q, k, v = (projected[:, j * width : (j + 1) * width] for j in range(3))
    key_valid = iota((1, rows), 1) < limit
    gathers2 = relays(ctxl, ctxf, 1)
    half_low = iota((half, width), 1) < HEAD
    key_heads = (k * low_b, k * high_b)
    for span, gather in zip(spans, gathers2):
        contexts = []
        for h in range(2):
            score = jnp.where(key_valid, 0.125 * dot_nt(q[span], key_heads[h]), MASKED)
            score = jnp.exp(score - jnp.max(score, axis=-1, keepdims=True))
            prob = score / jnp.sum(score, axis=-1, keepdims=True)
            vprobs[h, span, :] = prob
            contexts.append(dot_nn(prob.astype(BF16), v))
        ctxl[span, :] = jnp.where(half_low, contexts[0], contexts[1]).astype(BF16)
        gather.start()

    reduces2 = [
        PairReduce(
            tp, part2.at[j], pair2.at[j], joined2.at[j], got2.at[j], ex_send.at[j], ex_recv.at[j]
        )
        for j in range(2)
    ]
    own = pl.ds(pl.multiple_of(tp.me * width, width), width)
    for j, span in enumerate(spans):
        gathers2[j].finish()
        attention = dot_nn(side_by_side(ctxf.at[j]), outf[...].reshape(nt * width, nt * width))
        residual = side_by_side(visitf.at[j]).astype(F32) + attention
        scaled, inverse, normed = norm_rows(residual, gain2[...])
        rgrad[span, :] = residual
        scaled2[span, :] = scaled
        inverse2[span, :] = jnp.broadcast_to(inverse, (half, width))
        upper = dot_nn(normed, up[...])
        if j:
            reduces2[0].middle()
        bend = jnp.tanh(0.7978845608028654 * (upper + 0.044715 * upper * upper * upper))
        hidden[span, :] = (0.5 * upper * (1.0 + bend)).astype(BF16)
        slope = 0.5 * (1.0 + bend) + 0.5 * upper * (1.0 - bend * bend) * (
            0.7978845608028654 * (1.0 + 3.0 * 0.044715 * upper * upper)
        )
        upper_grad = (hidden_grad[span, :] * slope).astype(BF16)
        for x in range(nt // 2):
            pair = dot_nt(upper_grad, up[2 * x * width : 2 * (x + 1) * width, :]).astype(BF16)
            part2[j, 2 * x] = pair[:, :width]
            part2[j, 2 * x + 1] = pair[:, width:]
            reduces2[j].start(x)
    reduces2[1].middle()
    residual_own[...] = rgrad[:, own]
    gathers3 = relays(sum2, sum2f, 2)
    for span, reduce, gather in zip(spans, reduces2, gathers3):
        sum2[span, :] = reduce.finish().astype(BF16)
        gather.start()
    for j, span in enumerate(spans):
        gathers3[j].finish()
        weighted = side_by_side(sum2f.at[j]).astype(F32) * gain2[...]
        centred = weighted - jnp.mean(weighted, axis=-1, keepdims=True)
        given = jnp.concatenate([cotf[t, span, :] for t in range(nt)], axis=1).astype(F32)
        row = iota((half, nt * width), 0) + j * half
        scaled = scaled2[span, :]
        residual_grad = jnp.where(row < limit, given, 0.0) + inverse2[span, 0:1] * (
            centred - scaled * jnp.mean(weighted * scaled, axis=-1, keepdims=True)
        )
        rgrad[span, :] = residual_grad
        context_grads[span, :] = dot_nt(residual_grad.astype(BF16), outw[...]).astype(BF16)

    q, k, v = (projected[:, j * width : (j + 1) * width] for j in range(3))
    context_grad = context_grads[...]
    row_low = iota((rows, width), 1) < HEAD
    query_grads, key_grads, value_grads = [], [], []
    for h, mask in enumerate((low_b, high_b)):
        prob = vprobs[h]
        weight_grad = dot_nt(context_grad, v * mask)
        value_grads.append(dot_tn(prob.astype(BF16), context_grad))
        score_grad = (
            0.125 * prob * (weight_grad - jnp.sum(weight_grad * prob, axis=-1, keepdims=True))
        ).astype(BF16)
        query_grads.append(dot_nn(score_grad, k))
        key_grads.append(dot_tn(score_grad, q))
    packed = jnp.concatenate(
        [
            jnp.where(row_low, pair[0], pair[1]).astype(BF16)
            for pair in (query_grads, key_grads, value_grads)
        ],
        axis=1,
    )
    first_sum = jnp.zeros((rows, 1), F32)
    second_sum = jnp.zeros((rows, 1), F32)
    reduce1 = PairReduce(tp, part1, pair1, joined1, got1, ex_send.at[2], ex_recv.at[2])
    for x in range(nt // 2):
        cols = slice(2 * x * width, 2 * (x + 1) * width)
        partial = dot_nt(packed, qkv[cols, :])
        part1[2 * x] = partial[:, :width].astype(BF16)
        part1[2 * x + 1] = partial[:, width:].astype(BF16)
        reduce1.start(x)
    reduce1.middle()
    for t in range(nt):
        cols = slice(t * width, (t + 1) * width)
        weighted = part1[t].astype(F32) * gain1[:, cols]
        first_sum = first_sum + jnp.sum(weighted, axis=-1, keepdims=True)
        second_sum = second_sum + jnp.sum(weighted * scaled1[:, cols], axis=-1, keepdims=True)
    lane = iota((rows, width), 1)
    both_sums = jnp.where(lane == 0, first_sum, jnp.where(lane == 1, second_sum, 0.0))
    stat[...] = jnp.transpose(
        jnp.concatenate([both_sums, jnp.zeros((padded - rows, width), F32)], axis=0)
    )[:8]
    gather4 = Exchange(tp, stat, stats, stat_send, stat_recv, same=True)
    gather4.start()
    total = reduce1.finish()
    gather4.finish()
    means = stats[0]
    for t in range(1, nt):
        means = means + stats[t]
    means = jnp.transpose(
        jnp.concatenate([means, jnp.zeros((width - 8, padded), F32)], axis=0)
    )[:rows] * (1.0 / (nt * width))
    visit_grad = rgrad[:, own] + inverse1[...] * (
        total * gain1[:, own] - means[:, 0:1] - scaled1[:, own] * means[:, 1:2]
    )
    visit_grad = visit_grad.astype(BF16)
    slots2[...] = dot_nn(place_t[:, :rows], visit_grad).astype(BF16).reshape(nn, lat, width)
    back = AllToAll(nn, slots2, arrived2, a2a_send.at[2], a2a_recv.at[2])
    back.start()

    reducef = PairReduce(tp, partf, pairf, joinedf, gotf, ex_send.at[3], ex_recv.at[3])
    for x in range(nt // 2):
        pair = dot_nn(hidden[...], down[:, 2 * x * width : 2 * (x + 1) * width]).astype(BF16)
        partf[2 * x] = pair[:, :width]
        partf[2 * x + 1] = pair[:, width:]
        reducef.start(x)
    reducef.middle()
    column = iota((notes * lat, 1), 0)
    wanted = lax.rem(column, lat)
    for n in range(notes):
        wanted = jnp.where(column // lat == n, wanted + pid[n] * lat, wanted)
    unselect = (iota((notes * lat, nn * lat), 1) == wanted).astype(F32).astype(BF16)
    total = reducef.finish()
    visit_out[...] = jnp.where(row_valid, residual_own[...] + total, 0.0).astype(BF16)
    for one in gathers1 + gathers2 + gathers3 + reduces2 + [reduce1, reducef, gather4]:
        one.drain()

    back.finish()
    latent = dot_nn(unselect, arrived2[...].reshape(nn * lat, width)).astype(BF16)
    latent_out[...] = latent
    halves = (latent * low_b, latent * high_b)
    spread = jnp.concatenate(
        [half[n * lat : (n + 1) * lat] for n in range(notes) for half in halves], axis=0
    )
    partial = dot_nn(mixture[...], spread).astype(BF16)
    vpart[...] = partial.reshape(nz, ny, lat, width)
    y_copies = []

    def along_y(i, block, slots_y):
        for s in range(1, ny):
            to = lax.rem(wy + s, ny)
            one = remote(
                block(to),
                slots_y.at[wy],
                y_send.at[i, s],
                y_recv.at[i, wy],
                {"notes": wz * ny + to},
            )
            one.start()
            y_copies.append(one)

    def from_y(i, s, block, slots_y):
        owner = lax.rem(wy + s, ny)
        remote(
            block(owner),
            slots_y.at[owner],
            y_send.at[i, s],
            y_recv.at[i, owner],
            {"notes": wz * ny + owner},
        ).wait_recv()
        return slots_y[owner].astype(F32)

    def along_z(i, block, slots_z):
        def step(j, carry):
            to = lax.rem(wz + nz // 2 + (j + 1) // 2 * (1 - 2 * lax.rem(j, 2)), nz)
            device = {"notes": to * ny + wy}
            remote(block(to), slots_z.at[wz], z_send.at[i], z_recv.at[i], device).start()
            return carry

        lax.fori_loop(0, nz - 1, step, 0)

    def value_block(to):
        return vpart.at[:, to]

    def query_block(to):
        return qpart

    along_y(0, value_block, vgot)
    query_total = jnp.zeros((both, width), F32)
    for n in range(notes):
        here = slice(n * both, (n + 1) * both)
        tokens = slice(n * tok, (n + 1) * tok)
        prob = probs[here, :]
        prob_grad = dot_nt(spread[here], values[tokens, :])
        score_grad = prob * (prob_grad - jnp.sum(prob_grad * prob, axis=-1, keepdims=True))
        query_total = query_total + dot_nn(score_grad.astype(BF16), states[tokens, :])
    qpart[...] = 0.125 * jnp.where(lane_low, query_total[:lat], query_total[lat:])

    along_y(1, query_block, qgot)
    total = vpart[:, wy].astype(F32)
    for s in range(1, ny):
        total = total + from_y(0, s, value_block, vgot)
    vpart2[...] = total.astype(BF16)
    along_z(0, lambda to: vpart2.at[to], vgot2)
    query_sum = qpart[...]
    for s in range(1, ny):
        query_sum = query_sum + from_y(1, s, query_block, qgot)
    qpart2[...] = query_sum.astype(BF16)
    along_z(1, lambda to: qpart2, qgot2)
    vgot2[wz] = vpart2[wz]
    qgot2[wz] = qpart2[...]
    for one in y_copies:
        one.wait_send()
    span = pl.ds(0, nz - 1)
    remote(vpart2.at[span], vgot2.at[span], z_send.at[0], z_recv.at[0], {"notes": who}).wait()
    remote(qgot2.at[span], qgot2.at[span], z_send.at[1], z_recv.at[1], {"notes": who}).wait()
    total = vgot2[0].astype(F32)
    query_sum = qgot2[0].astype(F32)
    for z in range(1, nz):
        total = total + vgot2[z].astype(F32)
        query_sum = query_sum + qgot2[z].astype(F32)
    value_out[...] = total
    query_out[...] = query_sum


def hand_over(a, b, c, d, a_out, b_out, c_out, d_out):
    for src, dst in ((a, a_out), (b, b_out), (c, c_out), (d, d_out)):
        dst[...] = src[...]


def shards(
    mesh_shape,
    states,
    value_weight,
    latent_query,
    patient_ids,
    note_order,
    history_length,
    position_table,
    attention_gain,
    feedforward_gain,
    qkv_weight,
    out_weight,
    up_weight,
    down_weight,
    cotangent,
):
    nn, nt = mesh_shape["notes"], mesh_shape["tensor"]
    ny = 4
    nz = nn // ny
    notes, tok, width = states.shape
    lat, most = latent_query.shape[0], position_table.shape[0]
    rows = most * lat
    dim = nt * width
    inner = up_weight.shape[1]
    padded = -(-rows // 128) * 128
    both = 2 * lat
    dims = (nn, ny, nt, notes, tok, lat, most)
    vmem = pl.BlockSpec(memory_space=pltpu.VMEM)
    smem = pl.BlockSpec(memory_space=pltpu.SMEM)
    hbm = pl.BlockSpec(memory_space=pl.ANY)
    V = pltpu.VMEM
    dma = pltpu.SemaphoreType.DMA
    block = (nt, rows, width)
    halves = (2, nt, rows // 2, width)
    nx = nt // 2
    scratch = [
        V((notes * tok, width), BF16),
        V((lat, width), BF16),
        V((most, width), BF16),
        V((1, dim), F32),
        V((1, dim), F32),
        V((rows, width), BF16),
        V((width, dim), BF16),
        V((dim, width), BF16),
        V((dim, 3 * width), BF16),
        V((dim, inner), BF16),
        V((inner, dim), BF16),
        V((nt, notes * tok, width), BF16),
        V(block, BF16),
        V((nt, width, dim), BF16),
        V((nn, 1, width), I32),
        V((nn, 1, width), I32),
        V((notes * both, tok), F32),
        V((notes * both, tok), BF16),
        V((notes * tok, width), BF16),
        V((dim, notes * both), BF16),
        V((nn, lat, width), BF16),
        V((nn, lat, width), BF16),
        V((nn * lat, padded), BF16),
        V((padded, nn * lat), BF16),
        V((rows, width), BF16),
        V(halves, BF16),
        V((rows, dim), F32),
        V((rows, width), F32),
        V((rows, 3 * width), BF16),
        V((2, rows, rows), F32),
        V((rows, width), BF16),
        V(halves, BF16),
        V((rows, width), F32),
        V((rows, dim), F32),
        V((rows, width), F32),
        V((rows, inner), BF16),
        V((rows, inner), F32),
        V(halves, BF16),
        V((2, nx, rows // 2, width), BF16),
        V((2, nx - 1, rows // 2, width), BF16),
        V((2, nx, rows // 2, width), BF16),
        V((rows, width), BF16),
        V(halves, BF16),
        V((rows, width), BF16),
        V(block, BF16),
        V((nx, rows, width), BF16),
        V((nx - 1, rows, width), BF16),
        V((nx, rows, width), BF16),
        V((rows, dim), F32),
        V(block, BF16),
        V((nx, rows, width), BF16),
        V((nx - 1, rows, width), BF16),
        V((nx, rows, width), BF16),
        V((8, padded), F32),
        V((nt, 8, padded), F32),
        V((nn, lat, width), BF16),
        V((nn, lat, width), BF16),
        V((nz, ny, lat, width), BF16),
        V((ny, nz, lat, width), BF16),
        V((nz, lat, width), BF16),
        V((nz, lat, width), BF16),
        V((lat, width), F32),
        V((ny, lat, width), F32),
        V((lat, width), BF16),
        V((nz, lat, width), BF16),
        dma((13,)),
        dma((3, 14)),
        dma((3, nt, 2)),
        dma((3, 2, 7)),
        dma((3, 2, nt)),
        dma((4, nt - 1)),
        dma((4, nt)),
        dma((nt - 1,)),
        dma((nt,)),
        dma((3,)),
        dma((3,)),
        dma((2, ny)),
        dma((2, ny)),
        dma((2,)),
        dma((2,)),
    ]
    visit_out, latent_grads, value_grad, query_grad = pl.pallas_call(
        functools.partial(body, dims),
        out_shape=(
            jax.ShapeDtypeStruct((rows, width), BF16),
            jax.ShapeDtypeStruct((notes * lat, width), BF16),
            jax.ShapeDtypeStruct((dim // nn, width), F32),
            jax.ShapeDtypeStruct((lat, width), F32),
        ),
        in_specs=[smem] * 3 + [hbm] * 11,
        out_specs=(vmem,) * 4,
        scratch_shapes=scratch,
        name="note_visit_step",
        compiler_params=pltpu.CompilerParams(
            collective_id=0, has_side_effects=True, vmem_limit_bytes=56 * 2**20
        ),
    )(
        patient_ids,
        note_order,
        history_length,
        states.reshape(notes * tok, width),
        latent_query,
        position_table,
        attention_gain.reshape(1, dim),
        feedforward_gain.reshape(1, dim),
        cotangent.reshape(rows, width),
        out_weight,
        value_weight,
        jnp.transpose(qkv_weight, (1, 0, 2)),
        up_weight,
        down_weight,
    )
    results = (visit_out, latent_grads, value_grad, query_grad)
    visit_out, latent_grads, value_grad, query_grad = pl.pallas_call(
        hand_over,
        out_shape=tuple(jax.ShapeDtypeStruct(r.shape, r.dtype) for r in results),
        in_specs=[vmem] * 4,
        out_specs=(vmem,) * 4,
        name="hand_over",
    )(*results)
    return (
        visit_out[None],
        latent_grads.reshape(notes, lat, width),
        value_grad,
        query_grad,
    )


def solution(mesh):
    return jax.shard_map(
        functools.partial(shards, dict(mesh.shape)),
        mesh=mesh,
        in_specs=(
            P("notes", None, "tensor"),
            P(None, "tensor"),
            P(None, "tensor"),
            P("notes"),
            P("notes"),
            P("notes"),
            P(None, "tensor"),
            P(),
            P(),
            P(None, None, "tensor"),
            P("tensor", None),
            P(None, "tensor"),
            P("tensor", None),
            P("notes", None, "tensor"),
        ),
        out_specs=(
            P("notes", None, "tensor"),
            P("notes", None, "tensor"),
            P("notes", "tensor"),
            P(None, "tensor"),
        ),
        check_vma=False,
    )
```
